32 devices in a mesh: batch: 4 (over y, x), proto: 8 (over z, core).
Axes of the slice: x: 2, y: 2, z: 4, core: 2. Of those that a mesh axis runs over, the one named last changes fastest.
Arguments:
- features: bfloat16 [2048, 256], P('batch'), may hold values from -6 to 6
- prototypes: bfloat16 [16384, 256], P(('proto', 'batch')), may hold values from -6 to 6
Outputs:
- assignments: bfloat16 [2048, 16384], P('batch', 'proto')
The draws below stay inside these ranges and needn't reach their ends.
All inputs are finite; a program needn't handle non-finite values.
Results may differ from the reference program's by a relative error of at most 0.0061.
Values may be sent and summed in bfloat16 or wider, within the bound.
No kernel may reach another device: no remote copies, remote signals or barrier semaphores. Data moves between devices by JAX's collectives and lax.ppermute only.
A program may use at most 64 MiB of HBM per device.

```python
import jax
import jax.numpy as jnp
from jax import lax

D = 256
ITERS = 3
B = 2048
K = 16384


def cluster_centres(key):
    return jax.random.truncated_normal(jax.random.fold_in(key, 7), -3.0, 3.0, (16, D), jnp.float32)


def cluster_labels(key, row_total, reverse):
    bounds = jnp.array([303, 454, 555, 631, 692, 742, 785, 823, 857, 887, 915, 940, 963, 985, 1005], jnp.int32)
    ticket = jax.random.randint(key, (row_total,), 0, 1024, jnp.int32)
    labels = jnp.sum((ticket[:, None] >= bounds[None, :]).astype(jnp.int32), axis=1)
    if reverse:
        return 15 - labels
    return labels


def draw_features(key, part):
    centres = cluster_centres(key)
    labels = cluster_labels(jax.random.fold_in(key, 11), B, False)
    noise = jax.random.truncated_normal(jax.random.fold_in(key, 13), -3.0, 3.0, (B, D), jnp.float32)
    strength = 0.58
    return (strength * centres[labels] + noise).astype(jnp.bfloat16)


def draw_prototypes(key, part):
    centres = cluster_centres(key)
    labels = cluster_labels(jax.random.fold_in(key, 17), K, True)
    noise = jax.random.truncated_normal(jax.random.fold_in(key, 19), -3.0, 3.0, (K, D), jnp.float32)
    strength = 0.58
    return (strength * centres[labels] + noise).astype(jnp.bfloat16)


def setup_inputs(seed: int = 0) -> dict:
    key_list = jax.random.split(jax.random.key(seed), 3)
    return {
        "features": draw_features(jax.random.fold_in(key_list[2], 71), 0),
        "prototypes": draw_prototypes(jax.random.fold_in(key_list[2], 71), 0),
    }


def unit_rows(matrix):
    values = matrix.astype(jnp.float32)
    scale = jax.lax.rsqrt(1e-06 + lax.optimization_barrier(jnp.sum(values * values, axis=1, keepdims=True)))
    return (values * scale).astype(jnp.bfloat16)

def reference(features, prototypes):
    unit_feat = unit_rows(features)
    unit_proto = unit_rows(prototypes)
    scores = jnp.dot(unit_feat, unit_proto.T, preferred_element_type=jnp.float32)
    weights = jnp.exp(20.0 * scores)
    for step in range(ITERS):
        weights = weights / lax.optimization_barrier(jnp.sum(weights, axis=0, keepdims=True))
        weights = weights / lax.optimization_barrier(jnp.sum(weights, axis=1, keepdims=True))
    return (float(K) * weights).astype(jnp.bfloat16)
```

```python
import jax
import jax.numpy as jnp
from jax import lax
from jax.sharding import PartitionSpec as P

ITERS = 3
MOST_PARTNERS = 8


def unit_rows(matrix):
    values = matrix.astype(jnp.float32)
    scale = lax.rsqrt(1e-06 + jnp.sum(values * values, axis=1, keepdims=True))
    return (values * scale).astype(jnp.bfloat16)


def partners(size, stride, count, step):
    pairs = []
    for index in range(size):
        place = index // stride % count
        other = place ^ step if count & (count - 1) == 0 else (place + step) % count
        pairs.append((index, index + (other - place) * stride))
    return pairs


def from_others(value, axis, stride, count):
    size = lax.axis_size(axis)
    return [lax.ppermute(value, axis, partners(size, stride, count, step)) for step in range(1, count)]


def group_sum(value, axis, stride, count):
    total = value
    for other in from_others(value, axis, stride, count):
        total = total + other
    return total


def proto_sums(partial_value):
    size = lax.axis_size("batch")
    if size > MOST_PARTNERS:
        return lax.psum(partial_value, "batch")
    return group_sum(partial_value, "batch", 1, size)


def image_sums(partial_value):
    size = lax.axis_size("proto")
    if size > 2 * MOST_PARTNERS or size % 2:
        return lax.psum(partial_value, "proto")
    pair = group_sum(partial_value, "proto", 1, 2)
    return group_sum(pair, "proto", 2, size // 2)


def gather_prototypes(unit_proto):
    size = lax.axis_size("batch")
    if size > MOST_PARTNERS:
        return lax.all_gather(unit_proto, "batch", axis=0, tiled=True)
    blocks = [unit_proto] + from_others(unit_proto, "batch", 1, size)
    place = lax.axis_index("batch")
    order = [jnp.bitwise_xor(place, step) if size & (size - 1) == 0 else (place - step) % size for step in range(size)]
    gathered = jnp.zeros((size,) + unit_proto.shape, unit_proto.dtype)
    for index, block in zip(order, blocks):
        gathered = lax.dynamic_update_index_in_dim(gathered, block, index, 0)
    return gathered.reshape(-1, unit_proto.shape[1])


def local(features, prototypes):
    unit_feat = unit_rows(features)
    scores = jnp.einsum(
        "bd,kd->bk",
        unit_feat,
        gather_prototypes(unit_rows(prototypes)),
        preferred_element_type=jnp.float32,
    )
    weights = jnp.exp(20.0 * scores)
    total_protos = float(weights.shape[1] * lax.axis_size("proto"))
    row_factor = jnp.ones((weights.shape[0],), jnp.float32)
    col_factor = jnp.ones((weights.shape[1],), jnp.float32)
    for step in range(ITERS):
        column_part = jnp.dot(row_factor, weights, precision=lax.Precision.HIGHEST)
        col_factor = 1.0 / proto_sums(column_part)
        row_part = jnp.dot(weights, col_factor, precision=lax.Precision.HIGHEST)
        row_factor = 1.0 / image_sums(row_part)
    scaled = weights * row_factor[:, None] * (total_protos * col_factor)[None, :]
    return scaled.astype(jnp.bfloat16)


def solution(mesh):
    in_specs = (P("batch", None), P(("proto", "batch"), None))
    out_specs = P("batch", "proto")
    return jax.shard_map(local, mesh=mesh, in_specs=in_specs, out_specs=out_specs, check_vma=False)
```

```python
import functools

import jax
import jax.numpy as jnp
from jax import lax
from jax.experimental import pallas as pl
from jax.experimental.pallas import tpu as pltpu
from jax.sharding import PartitionSpec as P

ITERS = 3
MOST_PARTNERS = 8
BLOCK_BYTES = 20 * 2**20
VMEM = pltpu.VMEM
IN_VMEM = pl.BlockSpec(memory_space=pltpu.VMEM)
F32 = jnp.float32
LANES = 128


def unit_rows(matrix):
    values = matrix.astype(F32)
    scale = lax.rsqrt(1e-06 + jnp.sum(values * values, axis=1, keepdims=True))
    return (values * scale).astype(jnp.bfloat16)


def partners(size, stride, count, step):
    pairs = []
    for index in range(size):
        place = index // stride % count
        other = place ^ step if count & (count - 1) == 0 else (place + step) % count
        pairs.append((index, index + (other - place) * stride))
    return pairs


def from_others(value, axis, stride, count):
    size = lax.axis_size(axis)
    return [lax.ppermute(value, axis, partners(size, stride, count, step)) for step in range(1, count)]


def swap_cores(value):
    return lax.ppermute(value, "proto", partners(lax.axis_size("proto"), 1, 2, 1))


def group_sum(value, axis, stride, count):
    total = value
    for other in from_others(value, axis, stride, count):
        total = total + other
    return total


def proto_sums(partial_value):
    size = lax.axis_size("batch")
    if size > MOST_PARTNERS:
        return lax.psum(partial_value, "batch")
    return group_sum(partial_value, "batch", 1, size)


def image_sums(partial_value):
    size = lax.axis_size("proto")
    if size > 2 * MOST_PARTNERS or size % 2:
        return lax.psum(partial_value, "proto")
    pair = group_sum(partial_value, "proto", 1, 2)
    return group_sum(pair, "proto", 2, size // 2)


def split_plan(features, prototypes):
    unit_feat = unit_rows(features)
    gathered = lax.all_gather(unit_rows(prototypes), "batch", axis=0, tiled=True)
    scores = jnp.einsum("bd,kd->bk", unit_feat, gathered, preferred_element_type=F32)
    weights = jnp.exp(20.0 * scores)
    total_protos = float(weights.shape[1] * lax.axis_size("proto"))
    row_factor = jnp.ones((weights.shape[0],), F32)
    col_factor = jnp.ones((weights.shape[1],), F32)
    for step in range(ITERS):
        column_part = jnp.dot(row_factor, weights, precision=lax.Precision.HIGHEST)
        col_factor = 1.0 / proto_sums(column_part)
        row_part = jnp.dot(weights, col_factor, precision=lax.Precision.HIGHEST)
        row_factor = 1.0 / image_sums(row_part)
    scaled = weights * row_factor[:, None] * (total_protos * col_factor)[None, :]
    return scaled.astype(jnp.bfloat16)


def call(kernel, outs, args, limit, scratch=(), flops=0, transcendentals=0):
    pinned = [pltpu.with_memory_space_constraint(arg, VMEM) for arg in args]
    moved = sum(arg.size * arg.dtype.itemsize for arg in args)
    return pl.pallas_call(
        kernel,
        out_shape=[VMEM(shape, dtype) for shape, dtype in outs],
        in_specs=[IN_VMEM] * len(pinned),
        out_specs=[IN_VMEM] * len(outs),
        scratch_shapes=list(scratch),
        compiler_params=pltpu.CompilerParams(vmem_limit_bytes=limit * 2**20),
        cost_estimate=pl.CostEstimate(flops=flops, bytes_accessed=moved, transcendentals=transcendentals),
    )(*pinned)


def scores_of(protos, images):
    return lax.dot_general(protos, images, (((1,), (1,)), ((), ())), preferred_element_type=F32)


def tiles(width):
    return [slice(start, start + LANES) for start in range(0, width, LANES)]


def image_parts(weights_ref, rows, col_factor, store, add):
    count = rows.stop - rows.start
    factor = jnp.broadcast_to(col_factor, (count, LANES))
    for tile in tiles(weights_ref.shape[1]):
        product = weights_ref[rows, tile] * factor
        part = jnp.sum(jnp.sum(product.reshape(count // 8, 8, LANES), axis=0), axis=0, keepdims=True)
        store[:, tile] = store[:, tile] + part if add else part


def first_kernel(others, *refs):
    own, fetched, swapped = refs[0], refs[1 : 1 + others], refs[1 + others : 1 + 2 * others]
    protos, unit_feat, unit_proto, weights, part = refs[1 + 2 * others :]
    block = own.shape[0]
    half = block // 2
    core = lax.axis_index("proto") % 2
    unit_proto[...] = unit_rows(protos[...])
    unit_feat[:block, :] = unit_rows(own[...])
    for index in range(others):
        base = (index + 1) * block
        mine = pl.multiple_of(base + core * half, half)
        theirs = pl.multiple_of(base + (1 - core) * half, half)
        unit_feat[pl.ds(mine, half), :] = unit_rows(fetched[index][...])
        unit_feat[pl.ds(theirs, half), :] = unit_rows(swapped[index][...])
    rows = slice(0, protos.shape[0])
    total = jnp.zeros((rows.stop, LANES), F32)
    step = 2 * LANES
    for start in range(0, weights.shape[1], step):
        values = jnp.exp(20.0 * scores_of(unit_proto[...], unit_feat[start : start + step, :]))
        weights[:, start : start + step] = values
        for tile in tiles(step):
            total = total + values[:, tile]
    image_parts(weights, rows, 1.0 / jnp.sum(total, axis=1, keepdims=True), part, False)


def more_kernel(others, *refs):
    protos, unit_feat, unit_proto, weights = refs[:others], *refs[others:]
    block = protos[0].shape[0]
    for index in range(others):
        unit_proto[index * block : (index + 1) * block, :] = unit_rows(protos[index][...])
    step = 4 * LANES

    def body(index, carry):
        columns = pl.ds(pl.multiple_of(index * step, step), step)
        weights[:, columns] = jnp.exp(20.0 * scores_of(unit_proto[...], unit_feat[columns, :]))
        return carry

    lax.fori_loop(0, weights.shape[1] // step, body, 0)


def summed(parts, steps, block):
    total = parts[0][...]
    for part, step in zip(parts[1:], steps):
        value = part[...]
        if step:
            order = [index ^ step for index in range(value.shape[1] // block)]
            value = jnp.concatenate([value[:, i * block : (i + 1) * block] for i in order], axis=1)
        total = total + value
    return total


def pass_kernel(steps, block, *refs):
    count = len(steps) + 1
    parts, weights, (part, col_factor) = refs[:count], refs[count:-2], refs[-2:]
    row_factor = 1.0 / summed(parts, steps, block)
    base = 0
    for matrix in weights:
        height = matrix.shape[0]
        for start in range(0, height, block):
            rows = slice(start, start + block)
            total = jnp.zeros((block, LANES), F32)
            for tile in tiles(matrix.shape[1]):
                total = total + matrix[rows, tile] * row_factor[:, tile]
            factor = 1.0 / jnp.sum(total, axis=1, keepdims=True)
            col_factor[base + start : base + start + block, :] = jnp.broadcast_to(factor, (block, LANES))
            image_parts(matrix, rows, factor, part, base + start > 0)
        base += height


def ready_kernel(scale, unit_feat, own_proto, more_proto, col_factor, ready):
    block = ready.shape[0]
    images = unit_feat[:block, :]
    for start in range(0, ready.shape[1], block):
        protos = own_proto[...] if start == 0 else more_proto[start - block : start, :]
        values = jnp.exp(20.0 * scores_of(images, protos))
        for tile in tiles(block):
            at = slice(start + tile.start, start + tile.stop)
            factor = scale * jnp.transpose(col_factor[at, :])[:1, :]
            ready[:, at] = values[:, tile] * factor


def last_kernel(steps, block, *refs):
    count = len(steps) + 1
    parts, ready, out, staged, sems = refs[:count], *refs[count:]
    total = summed(parts, steps, block)
    factors = []
    for tile in tiles(block):
        factors.append(jnp.transpose(jnp.broadcast_to(1.0 / total[:, tile], (LANES, LANES))))
    factor = jnp.concatenate(factors, axis=0)
    place = lax.axis_index("batch")
    copies = []
    for index in range(ready.shape[1] // block):
        for tile in tiles(block):
            at = slice(tile.start, tile.stop)
            values = ready[:, index * block + tile.start : index * block + tile.stop]
            staged[index, :, at] = (values * factor).astype(staged.dtype)
        column = pl.multiple_of(jnp.bitwise_xor(place, index) * block, block)
        copies.append(pltpu.make_async_copy(staged.at[index], out.at[:, pl.ds(column, block)], sems.at[index]))
        copies[-1].start()
    for copy in copies:
        copy.wait()


def whole_plan(features, prototypes):
    bf16 = jnp.bfloat16
    blocks = lax.axis_size("batch")
    others = blocks - 1
    block, depth = features.shape
    height = prototypes.shape[0]
    images = blocks * block
    z_count = lax.axis_size("proto") // 2
    total_protos = float(height * blocks * lax.axis_size("proto"))

    core = lax.axis_index("proto") % 2
    mine = lax.dynamic_slice_in_dim(features, core * (block // 2), block // 2, 0)
    fetched = from_others(mine, "batch", 1, blocks)
    swapped = [swap_cores(value) for value in fetched]
    received = from_others(prototypes, "batch", 1, blocks)

    def around(value):
        pair = value + swap_cores(value)
        return [pair] + from_others(pair, "proto", 2, z_count)

    unit_feat, own_proto, own_weights, part = call(
        functools.partial(first_kernel, others),
        [((images, depth), bf16), ((height, depth), bf16), ((height, images), F32), ((1, images), F32)],
        [features, *fetched, *swapped, prototypes],
        16,
        flops=2 * height * images * depth,
        transcendentals=height * images,
    )
    chips = sum(around(part))
    chips, *received = lax.optimization_barrier((chips, *received))
    parts = [chips] + from_others(chips, "batch", 1, blocks)
    steps = list(range(1, blocks))
    more_proto, more_weights = call(
        functools.partial(more_kernel, others),
        [((others * height, depth), bf16), ((others * height, images), F32)],
        [*received, unit_feat],
        16,
        flops=2 * others * height * images * depth,
        transcendentals=others * height * images,
    )
    for step in range(1, ITERS):
        part, col_factor = call(
            functools.partial(pass_kernel, steps, block),
            [((1, images), F32), ((blocks * height, LANES), F32)],
            [*parts, own_weights, more_weights],
            8,
            flops=4 * blocks * height * images,
        )
        parts = around(part)
        steps = [0] * (z_count - 1)
    (ready,) = call(
        functools.partial(ready_kernel, total_protos),
        [((block, blocks * height), F32)],
        [unit_feat, own_proto, more_proto, col_factor],
        16,
        flops=2 * block * blocks * height * depth,
        transcendentals=block * blocks * height,
    )
    pinned = [pltpu.with_memory_space_constraint(arg, VMEM) for arg in [*parts, ready]]
    return pl.pallas_call(
        functools.partial(last_kernel, steps, block),
        out_shape=jax.ShapeDtypeStruct((block, blocks * height), bf16),
        in_specs=[IN_VMEM] * len(pinned),
        out_specs=pl.BlockSpec(memory_space=pl.ANY),
        scratch_shapes=[VMEM((blocks, block, height), bf16), pltpu.SemaphoreType.DMA((blocks,))],
        compiler_params=pltpu.CompilerParams(vmem_limit_bytes=8 * 2**20),
    )(*pinned)


def local(features, prototypes):
    blocks = lax.axis_size("batch")
    block, height = features.shape[0], prototypes.shape[0]
    fits = 4 * blocks * blocks * block * height <= BLOCK_BYTES
    even = block == height and block % (2 * LANES) == 0 and blocks & (blocks - 1) == 0
    if fits and even and lax.axis_size("proto") % 2 == 0 and lax.axis_size("proto") <= 2 * MOST_PARTNERS:
        return whole_plan(features, prototypes)
    return split_plan(features, prototypes)


def solution(mesh):
    in_specs = (P("batch", None), P(("proto", "batch"), None))
    out_specs = P("batch", "proto")
    return jax.shard_map(local, mesh=mesh, in_specs=in_specs, out_specs=out_specs, check_vma=False)
```

```python
import functools

import jax
import jax.numpy as jnp
from jax import lax
from jax.experimental import pallas as pl
from jax.experimental.pallas import tpu as pltpu
from jax.sharding import PartitionSpec as P

ITERS = 3
MOST_PARTNERS = 8
BLOCK_BYTES = 20 * 2**20
VMEM = pltpu.VMEM
IN_VMEM = pl.BlockSpec(memory_space=pltpu.VMEM)
F32 = jnp.float32
LANES = 128


def unit_rows(matrix):
    values = matrix.astype(F32)
    scale = lax.rsqrt(1e-06 + jnp.sum(values * values, axis=1, keepdims=True))
    return (values * scale).astype(jnp.bfloat16)


def partners(size, stride, count, step):
    pairs = []
    for index in range(size):
        place = index // stride % count
        other = place ^ step if count & (count - 1) == 0 else (place + step) % count
        pairs.append((index, index + (other - place) * stride))
    return pairs


def from_others(value, axis, stride, count):
    size = lax.axis_size(axis)
    return [lax.ppermute(value, axis, partners(size, stride, count, step)) for step in range(1, count)]


def swap_cores(value):
    return lax.ppermute(value, "proto", partners(lax.axis_size("proto"), 1, 2, 1))


def group_sum(value, axis, stride, count):
    total = value
    for other in from_others(value, axis, stride, count):
        total = total + other
    return total


def proto_sums(partial_value):
    size = lax.axis_size("batch")
    if size > MOST_PARTNERS:
        return lax.psum(partial_value, "batch")
    return group_sum(partial_value, "batch", 1, size)


def image_sums(partial_value):
    size = lax.axis_size("proto")
    if size > 2 * MOST_PARTNERS or size % 2:
        return lax.psum(partial_value, "proto")
    pair = group_sum(partial_value, "proto", 1, 2)
    return group_sum(pair, "proto", 2, size // 2)


def split_plan(features, prototypes):
    unit_feat = unit_rows(features)
    gathered = lax.all_gather(unit_rows(prototypes), "batch", axis=0, tiled=True)
    scores = jnp.einsum("bd,kd->bk", unit_feat, gathered, preferred_element_type=F32)
    weights = jnp.exp(20.0 * scores)
    total_protos = float(weights.shape[1] * lax.axis_size("proto"))
    row_factor = jnp.ones((weights.shape[0],), F32)
    col_factor = jnp.ones((weights.shape[1],), F32)
    for step in range(ITERS):
        column_part = jnp.dot(row_factor, weights, precision=lax.Precision.HIGHEST)
        col_factor = 1.0 / proto_sums(column_part)
        row_part = jnp.dot(weights, col_factor, precision=lax.Precision.HIGHEST)
        row_factor = 1.0 / image_sums(row_part)
    scaled = weights * row_factor[:, None] * (total_protos * col_factor)[None, :]
    return scaled.astype(jnp.bfloat16)


def call(kernel, outs, args, limit, cost=0, aliases=None, scratch=()):
    pinned = [pltpu.with_memory_space_constraint(arg, VMEM) for arg in args]
    return pl.pallas_call(
        kernel,
        out_shape=[VMEM(shape, dtype) for shape, dtype in outs],
        in_specs=[IN_VMEM] * len(pinned),
        out_specs=[IN_VMEM] * len(outs),
        input_output_aliases=aliases or {},
        scratch_shapes=list(scratch),
        compiler_params=pltpu.CompilerParams(vmem_limit_bytes=limit * 2**20),
        cost_estimate=pl.CostEstimate(flops=cost, bytes_accessed=0, transcendentals=0),
    )(*pinned)


def scores_of(protos, images):
    return lax.dot_general(protos, images, (((1,), (1,)), ((), ())), preferred_element_type=F32)


def tiles(width):
    return [slice(start, start + LANES) for start in range(0, width, LANES)]


def fill(weights, total, rows, columns, unit_proto, unit_feat):
    step = 2 * LANES
    for column in range(columns.start, columns.stop, step):
        values = jnp.exp(20.0 * scores_of(unit_proto, unit_feat[column : column + step, :]))
        weights[rows, column : column + step] = values
        for tile in tiles(step):
            total = total + values[:, tile]
    return total


def add_images(part, weights, rows, col_factor):
    count = col_factor.shape[0]
    for tile in tiles(weights.shape[1]):
        product = weights[rows, tile] * col_factor
        part[:, tile] = part[:, tile] + jnp.sum(product.reshape(count // 8, 8, LANES), axis=0)


def spread(lane_sums):
    return jnp.broadcast_to(1.0 / jnp.sum(lane_sums, axis=1, keepdims=True), lane_sums.shape)


def unit_kernel(*refs):
    half = len(refs) // 2
    for raw, unit in zip(refs[:half], refs[half:]):
        unit[...] = unit_rows(raw[...])


def near_kernel(own_feat, near, near_swapped, own_proto, first, unit_feat, unit_proto, weights, sums):
    block = own_feat.shape[0]
    core = lax.axis_index("proto") % 2
    unit_feat[:block, :] = own_feat[...]
    unit_feat[pl.ds(pl.multiple_of((1 + core) * block, block), block), :] = unit_rows(near[...])
    unit_feat[pl.ds(pl.multiple_of((2 - core) * block, block), block), :] = unit_rows(near_swapped[...])
    unit_proto[:block, :] = own_proto[...]
    unit_proto[block : 2 * block, :] = unit_rows(first[...])

    def body(index, carry):
        rows = pl.ds(pl.multiple_of(index * block, block), block)
        total = jnp.zeros((block, LANES), F32)
        sums[rows, :] = fill(weights, total, rows, slice(0, 3 * block), unit_proto[rows, :], unit_feat)
        return carry

    lax.fori_loop(0, 2, body, 0)


def far_kernel(far, far_swapped, sums, unit_proto, feat_in, weights_in, unit_feat, weights, part):
    half = far.shape[0]
    block = 2 * half
    core = lax.axis_index("proto") % 2
    unit_feat[pl.ds(pl.multiple_of(3 * block + (1 - core) * half, half), half), :] = unit_rows(far[...])
    unit_feat[pl.ds(pl.multiple_of(3 * block + core * half, half), half), :] = unit_rows(far_swapped[...])
    part[...] = jnp.zeros(part.shape, F32)

    def body(index, carry):
        rows = pl.ds(pl.multiple_of(index * block, block), block)
        total = fill(weights, sums[rows, :], rows, slice(3 * block, 4 * block), unit_proto[rows, :], unit_feat)
        add_images(part, weights, rows, spread(total))
        return carry

    lax.fori_loop(0, 2, body, 0)


def more_kernel(index, raw, unit_feat, proto_in, weights_in, part_in, unit_proto, weights, part, *row_sums):
    block = raw.shape[0]
    rows = slice(index * block, (index + 1) * block)
    unit_proto[rows, :] = unit_rows(raw[...])
    total = jnp.zeros((block, LANES), F32)
    total = fill(weights, total, rows, slice(0, 4 * block), unit_proto[rows, :], unit_feat)
    add_images(part, weights, rows, spread(total))
    for store in row_sums:
        store[...] = flat(part)


def flat(part):
    return jnp.sum(part[...], axis=0, keepdims=True)


def summed(parts):
    total = parts[0][...]
    for part in parts[1:]:
        total = total + part[...]
    return total


def pass_kernel(count, block, *refs):
    parts, weights, row_sums, *col_factor, part = refs[:count], *refs[count:]
    row_factor = 1.0 / summed(parts)
    part[...] = jnp.zeros(part.shape, F32)

    def body(index, carry):
        rows = pl.ds(pl.multiple_of(index * block, block), block)
        total = jnp.zeros((block, LANES), F32)
        for tile in tiles(weights.shape[1]):
            total = total + weights[rows, tile] * row_factor[:, tile]
        factor = spread(total)
        for store in col_factor:
            store[rows, :] = factor
        add_images(part, weights, rows, factor)
        return carry

    lax.fori_loop(0, weights.shape[0] // block, body, 0)
    row_sums[...] = flat(part)


def ready_kernel(scale, unit_feat, unit_proto, col_factor, ready):
    block = ready.shape[0]
    images = unit_feat[:block, :]
    for start in range(0, ready.shape[1], block):
        values = jnp.exp(20.0 * scores_of(images, unit_proto[start : start + block, :]))
        for tile in tiles(block):
            at = slice(start + tile.start, start + tile.stop)
            factor = scale * jnp.transpose(col_factor[at, :])[:1, :]
            ready[:, at] = values[:, tile] * factor


def last_kernel(count, block, *refs):
    parts, ready, out, staged, sems = refs[:count], *refs[count:]
    total = summed(parts)
    factors = []
    for tile in tiles(block):
        factors.append(jnp.transpose(jnp.broadcast_to(1.0 / total[:, tile], (LANES, LANES))))
    factor = jnp.concatenate(factors, axis=0)
    place = lax.axis_index("batch")
    core = lax.axis_index("proto") % 2
    copies = []
    for index, step in enumerate((0, 1 + core, 2 - core, 3)):
        for tile in tiles(block):
            values = ready[:, index * block + tile.start : index * block + tile.stop]
            staged[index, :, tile] = (values * factor).astype(staged.dtype)
        column = pl.multiple_of(jnp.bitwise_xor(place, step) * block, block)
        copies.append(pltpu.make_async_copy(staged.at[index], out.at[:, pl.ds(column, block)], sems.at[index]))
        copies[-1].start()
    for copy in copies:
        copy.wait()


def by_core(steps):
    protos, blocks = lax.axis_size("proto"), lax.axis_size("batch")
    return [
        (place * protos + proto, (place ^ steps[proto % 2]) * protos + proto)
        for place in range(blocks)
        for proto in range(protos)
    ]


def send(value, steps):
    return lax.ppermute(value, ("batch", "proto"), by_core(steps))


def whole_plan(features, prototypes):
    bf16 = jnp.bfloat16
    blocks = lax.axis_size("batch")
    block, depth = features.shape
    images = blocks * block
    z_count = lax.axis_size("proto") // 2
    total_protos = float(images * lax.axis_size("proto"))
    feat_shape = ((images, depth), bf16)
    weights_shape = ((images, images), F32)
    part_shape = ((8, images), F32)
    lanes_shape = ((images, LANES), F32)

    half = block // 2
    core = lax.axis_index("proto") % 2
    own_feat, own_proto = call(unit_kernel, [((block, depth), bf16)] * 2, [features, prototypes], 4)
    near = send(features, (1, 2))
    first = send(prototypes, (1, 2))
    later, own_proto = lax.optimization_barrier((prototypes, own_proto))
    second = send(later, (2, 1))
    near_half = lax.dynamic_slice_in_dim(near, (1 - core) * half, half, 0)
    forward, own_feat, own_proto = lax.optimization_barrier((near_half, own_feat, own_proto))
    far = send(forward, (2, 1))
    last = send(first, (2, 1))
    unit_feat, unit_proto, weights, sums = call(
        near_kernel,
        [feat_shape, feat_shape, weights_shape, lanes_shape],
        [own_feat, near, swap_cores(near), own_proto, first],
        16,
    )
    unit_feat, weights, part = call(
        far_kernel,
        [feat_shape, weights_shape, part_shape],
        [far, swap_cores(far), sums, unit_proto, unit_feat, weights],
        16,
        aliases={4: 0, 5: 1},
    )
    outs = [feat_shape, weights_shape, part_shape, ((1, images), F32)]
    for index, raw in ((2, second), (3, last)):
        unit_proto, weights, part, *row_sums = call(
            functools.partial(more_kernel, index),
            outs if index == 3 else outs[:3],
            [raw, unit_feat, unit_proto, weights, part],
            16,
            aliases={2: 0, 3: 1, 4: 2},
        )

    def around(value):
        total = value + swap_cores(value)
        for other in reversed(from_others(total, "proto", 2, z_count)):
            total = lax.optimization_barrier(total + other)
        return [total]

    parts = around(*row_sums)
    for step in range(1, ITERS):
        outs = [((1, images), F32), lanes_shape]
        row_sums, *col_factor = call(
            functools.partial(pass_kernel, len(parts), block),
            outs if step == ITERS - 1 else outs[:1],
            [*parts, weights],
            8,
            cost=4 * images * images,
            scratch=[VMEM(*part_shape)],
        )
        parts = around(row_sums)
    (ready,) = call(
        functools.partial(ready_kernel, total_protos),
        [((block, images), F32)],
        [unit_feat, unit_proto, *col_factor],
        16,
        cost=2 * block * images * depth,
    )
    pinned = [pltpu.with_memory_space_constraint(arg, VMEM) for arg in [*parts, ready]]
    return pl.pallas_call(
        functools.partial(last_kernel, len(parts), block),
        out_shape=jax.ShapeDtypeStruct((block, images), bf16),
        in_specs=[IN_VMEM] * len(pinned),
        out_specs=pl.BlockSpec(memory_space=pl.ANY),
        scratch_shapes=[VMEM((blocks, block, block), bf16), pltpu.SemaphoreType.DMA((blocks,))],
        compiler_params=pltpu.CompilerParams(vmem_limit_bytes=8 * 2**20),
    )(*pinned)


def local(features, prototypes):
    blocks = lax.axis_size("batch")
    block, height = features.shape[0], prototypes.shape[0]
    fits = 4 * blocks * blocks * block * height <= BLOCK_BYTES
    even = block == height and block % (2 * LANES) == 0 and blocks == 4
    if fits and even and lax.axis_size("proto") % 2 == 0 and lax.axis_size("proto") <= 2 * MOST_PARTNERS:
        return whole_plan(features, prototypes)
    return split_plan(features, prototypes)


def solution(mesh):
    in_specs = (P("batch", None), P(("proto", "batch"), None))
    out_specs = P("batch", "proto")
    return jax.shard_map(local, mesh=mesh, in_specs=in_specs, out_specs=out_specs, check_vma=False)
```

```python
import functools

import jax
import jax.numpy as jnp
from jax import lax
from jax.experimental import pallas as pl
from jax.experimental.pallas import tpu as pltpu
from jax.sharding import PartitionSpec as P

ITERS = 3
MOST_PARTNERS = 8
BLOCK_BYTES = 20 * 2**20
VMEM = pltpu.VMEM
IN_VMEM = pl.BlockSpec(memory_space=pltpu.VMEM)
F32 = jnp.float32
LANES = 128


def unit_rows(matrix):
    values = matrix.astype(F32)
    scale = lax.rsqrt(1e-06 + jnp.sum(values * values, axis=1, keepdims=True))
    return (values * scale).astype(jnp.bfloat16)


def partners(size, stride, count, step):
    pairs = []
    for index in range(size):
        place = index // stride % count
        other = place ^ step if count & (count - 1) == 0 else (place + step) % count
        pairs.append((index, index + (other - place) * stride))
    return pairs


def from_others(value, axis, stride, count):
    size = lax.axis_size(axis)
    return [lax.ppermute(value, axis, partners(size, stride, count, step)) for step in range(1, count)]


def swap_cores(value):
    return lax.ppermute(value, "proto", partners(lax.axis_size("proto"), 1, 2, 1))


def group_sum(value, axis, stride, count):
    total = value
    for other in from_others(value, axis, stride, count):
        total = total + other
    return total


def proto_sums(partial_value):
    size = lax.axis_size("batch")
    if size > MOST_PARTNERS:
        return lax.psum(partial_value, "batch")
    return group_sum(partial_value, "batch", 1, size)


def image_sums(partial_value):
    size = lax.axis_size("proto")
    if size > 2 * MOST_PARTNERS or size % 2:
        return lax.psum(partial_value, "proto")
    pair = group_sum(partial_value, "proto", 1, 2)
    return group_sum(pair, "proto", 2, size // 2)


def split_plan(features, prototypes):
    unit_feat = unit_rows(features)
    gathered = lax.all_gather(unit_rows(prototypes), "batch", axis=0, tiled=True)
    scores = jnp.einsum("bd,kd->bk", unit_feat, gathered, preferred_element_type=F32)
    weights = jnp.exp(20.0 * scores)
    total_protos = float(weights.shape[1] * lax.axis_size("proto"))
    row_factor = jnp.ones((weights.shape[0],), F32)
    col_factor = jnp.ones((weights.shape[1],), F32)
    for step in range(ITERS):
        column_part = jnp.dot(row_factor, weights, precision=lax.Precision.HIGHEST)
        col_factor = 1.0 / proto_sums(column_part)
        row_part = jnp.dot(weights, col_factor, precision=lax.Precision.HIGHEST)
        row_factor = 1.0 / image_sums(row_part)
    scaled = weights * row_factor[:, None] * (total_protos * col_factor)[None, :]
    return scaled.astype(jnp.bfloat16)


def call(kernel, outs, args, limit, cost=0, aliases=None, scratch=()):
    pinned = [pltpu.with_memory_space_constraint(arg, VMEM) for arg in args]
    return pl.pallas_call(
        kernel,
        out_shape=[VMEM(shape, dtype) for shape, dtype in outs],
        in_specs=[IN_VMEM] * len(pinned),
        out_specs=[IN_VMEM] * len(outs),
        input_output_aliases=aliases or {},
        scratch_shapes=list(scratch),
        compiler_params=pltpu.CompilerParams(vmem_limit_bytes=limit * 2**20),
        cost_estimate=pl.CostEstimate(flops=max(cost,1), bytes_accessed=1, transcendentals=1),
    )(*pinned)


def scores_of(protos, images):
    return lax.dot_general(protos, images, (((1,), (1,)), ((), ())), preferred_element_type=F32)


def tiles(width):
    return [slice(start, start + LANES) for start in range(0, width, LANES)]


def fill(weights, total, rows, columns, unit_proto, unit_feat):
    step = 2 * LANES
    for column in range(columns.start, columns.stop, step):
        values = jnp.exp(20.0 * scores_of(unit_proto, unit_feat[column : column + step, :]))
        weights[rows, column : column + step] = values
        for tile in tiles(step):
            total = total + values[:, tile]
    return total


def add_images(part, weights, rows, col_factor):
    count = col_factor.shape[0]
    for tile in tiles(part.shape[1]):
        product = weights[rows, tile] * col_factor
        part[:, tile] = part[:, tile] + jnp.sum(product.reshape(count // 8, 8, LANES), axis=0)


def spread(lane_sums):
    return jnp.broadcast_to(1.0 / jnp.sum(lane_sums, axis=1, keepdims=True), lane_sums.shape)


def unit_kernel(*refs):
    half = len(refs) // 2
    for raw, unit in zip(refs[:half], refs[half:]):
        unit[...] = unit_rows(raw[...])


def near_kernel(own_feat, near, near_swapped, own_proto, first, unit_feat, unit_proto, weights, sums):
    block = own_feat.shape[0]
    core = lax.axis_index("proto") % 2
    unit_feat[:block, :] = own_feat[...]
    unit_feat[pl.ds(pl.multiple_of((1 + core) * block, block), block), :] = unit_rows(near[...])
    unit_feat[pl.ds(pl.multiple_of((2 - core) * block, block), block), :] = unit_rows(near_swapped[...])
    unit_proto[:block, :] = own_proto[...]
    unit_proto[block : 2 * block, :] = unit_rows(first[...])

    def body(index, carry):
        rows = pl.ds(pl.multiple_of(index * block, block), block)
        total = jnp.zeros((block, LANES), F32)
        sums[rows, :] = fill(weights, total, rows, slice(0, 3 * block), unit_proto[rows, :], unit_feat)
        return carry

    lax.fori_loop(0, 2, body, 0)


def far_kernel(far, far_swapped, sums, unit_proto, feat_in, weights_in, unit_feat, weights, part):
    half = far.shape[0]
    block = 2 * half
    core = lax.axis_index("proto") % 2
    unit_feat[pl.ds(pl.multiple_of(3 * block + (1 - core) * half, half), half), :] = unit_rows(far[...])
    unit_feat[pl.ds(pl.multiple_of(3 * block + core * half, half), half), :] = unit_rows(far_swapped[...])
    part[...] = jnp.zeros(part.shape, F32)

    def body(index, carry):
        rows = pl.ds(pl.multiple_of(index * block, block), block)
        total = fill(weights, sums[rows, :], rows, slice(3 * block, 4 * block), unit_proto[rows, :], unit_feat)
        add_images(part, weights, rows, spread(total))
        return carry

    lax.fori_loop(0, 2, body, 0)


def more_kernel(index, raw, unit_feat, proto_in, weights_in, part_in, unit_proto, weights, part, *row_sums):
    block = raw.shape[0]
    rows = slice(index * block, (index + 1) * block)
    unit_proto[rows, :] = unit_rows(raw[...])
    total = jnp.zeros((block, LANES), F32)
    total = fill(weights, total, rows, slice(0, 4 * block), unit_proto[rows, :], unit_feat)
    add_images(part, weights, rows, spread(total))
    for store in row_sums:
        store[...] = flat(part)


def flat(part):
    return jnp.sum(part[...], axis=0, keepdims=True)


def summed(parts):
    total = parts[0][...]
    for part in parts[1:]:
        total = total + part[...]
    return total


def pass_kernel(count, block, *refs):
    parts, weights, row_sums, *col_factor, part = refs[:count], *refs[count:]
    row_factor = 1.0 / summed(parts)
    part[...] = jnp.zeros(part.shape, F32)

    def body(index, carry):
        rows = pl.ds(pl.multiple_of(index * block, block), block)
        total = jnp.zeros((block, LANES), F32)
        for tile in tiles(weights.shape[1]):
            total = total + weights[rows, tile] * row_factor[:, tile]
        factor = spread(total)
        for store in col_factor:
            store[rows, :] = factor
        add_images(part, weights, rows, factor)
        return carry

    lax.fori_loop(0, weights.shape[0] // block, body, 0)
    row_sums[...] = flat(part)


def ready_kernel(scale, unit_feat, unit_proto, col_factor, ready):
    block = ready.shape[0]
    images = unit_feat[:block, :]
    for start in range(0, ready.shape[1], block):
        values = jnp.exp(20.0 * scores_of(images, unit_proto[start : start + block, :]))
        for tile in tiles(block):
            at = slice(start + tile.start, start + tile.stop)
            factor = scale * jnp.transpose(col_factor[at, :])[:1, :]
            ready[:, at] = values[:, tile] * factor


def last_kernel(count, block, *refs):
    parts, ready, out, staged, sems = refs[:count], *refs[count:]
    total = summed(parts)
    factors = []
    for tile in tiles(block):
        factors.append(jnp.transpose(jnp.broadcast_to(1.0 / total[:, tile], (LANES, LANES))))
    factor = jnp.concatenate(factors, axis=0)
    place = lax.axis_index("batch")
    core = lax.axis_index("proto") % 2
    copies = []
    for index, step in enumerate((0, 1 + core, 2 - core, 3)):
        for tile in tiles(block):
            values = ready[:, index * block + tile.start : index * block + tile.stop]
            staged[index, :, tile] = (values * factor).astype(staged.dtype)
        column = pl.multiple_of(jnp.bitwise_xor(place, step) * block, block)
        copies.append(pltpu.make_async_copy(staged.at[index], out.at[:, pl.ds(column, block)], sems.at[index]))
        copies[-1].start()
    for copy in copies:
        copy.wait()


def by_core(steps):
    protos, blocks = lax.axis_size("proto"), lax.axis_size("batch")
    return [
        (place * protos + proto, (place ^ steps[proto % 2]) * protos + proto)
        for place in range(blocks)
        for proto in range(protos)
    ]


def send(value, steps):
    return lax.ppermute(value, ("batch", "proto"), by_core(steps))


def whole_plan(features, prototypes):
    bf16 = jnp.bfloat16
    blocks = lax.axis_size("batch")
    block, depth = features.shape
    images = blocks * block
    z_count = lax.axis_size("proto") // 2
    total_protos = float(images * lax.axis_size("proto"))
    feat_shape = ((images, depth), bf16)
    weights_shape = ((images, images), F32)
    part_shape = ((8, images), F32)
    lanes_shape = ((images, LANES), F32)

    half = block // 2
    core = lax.axis_index("proto") % 2
    own_feat, own_proto = call(unit_kernel, [((block, depth), bf16)] * 2, [features, prototypes], 4)
    near = send(features, (1, 2))
    first = send(prototypes, (1, 2))
    later, own_proto = lax.optimization_barrier((prototypes, own_proto))
    second = send(later, (2, 1))
    near_half = lax.dynamic_slice_in_dim(near, (1 - core) * half, half, 0)
    forward, own_feat, own_proto = lax.optimization_barrier((near_half, own_feat, own_proto))
    far = send(forward, (2, 1))
    last = send(first, (2, 1))
    unit_feat, unit_proto, weights, sums = call(
        near_kernel,
        [feat_shape, feat_shape, weights_shape, lanes_shape],
        [own_feat, near, swap_cores(near), own_proto, first],
        16,
    )
    unit_feat, weights, part = call(
        far_kernel,
        [feat_shape, weights_shape, part_shape],
        [far, swap_cores(far), sums, unit_proto, unit_feat, weights],
        16,
        aliases={4: 0, 5: 1},
    )
    outs = [feat_shape, weights_shape, part_shape, ((1, images), F32)]
    for index, raw in ((2, second), (3, last)):
        unit_proto, weights, part, *row_sums = call(
            functools.partial(more_kernel, index),
            outs if index == 3 else outs[:3],
            [raw, unit_feat, unit_proto, weights, part],
            16,
            aliases={2: 0, 3: 1, 4: 2},
        )

    def around(value):
        total = value + swap_cores(value)
        for other in reversed(from_others(total, "proto", 2, z_count)):
            total = lax.optimization_barrier(total + other)
        return [total]

    parts = around(*row_sums)
    for step in range(1, ITERS):
        final = step == ITERS - 1
        wanted = block if final else images
        row_sums, *col_factor = call(
            functools.partial(pass_kernel, len(parts), block),
            [((1, wanted), F32), lanes_shape] if final else [((1, wanted), F32)],
            [*parts, weights],
            8,
            cost=4 * images * images,
            scratch=[VMEM((8, wanted), F32)],
        )
        parts = around(row_sums)
    (ready,) = call(
        functools.partial(ready_kernel, total_protos),
        [((block, images), F32)],
        [unit_feat, unit_proto, *col_factor],
        16,
        cost=2 * block * images * depth,
    )
    pinned = [pltpu.with_memory_space_constraint(arg, VMEM) for arg in [*parts, ready]]
    return pl.pallas_call(
        functools.partial(last_kernel, len(parts), block),
        out_shape=jax.ShapeDtypeStruct((block, images), bf16),
        in_specs=[IN_VMEM] * len(pinned),
        out_specs=pl.BlockSpec(memory_space=pl.ANY),
        scratch_shapes=[VMEM((blocks, block, block), bf16), pltpu.SemaphoreType.DMA((blocks,))],
        compiler_params=pltpu.CompilerParams(vmem_limit_bytes=8 * 2**20),
    )(*pinned)


def local(features, prototypes):
    blocks = lax.axis_size("batch")
    block, height = features.shape[0], prototypes.shape[0]
    fits = 4 * blocks * blocks * block * height <= BLOCK_BYTES
    even = block == height and block % (2 * LANES) == 0 and blocks == 4
    if fits and even and lax.axis_size("proto") % 2 == 0 and lax.axis_size("proto") <= 2 * MOST_PARTNERS:
        return whole_plan(features, prototypes)
    return split_plan(features, prototypes)


def solution(mesh):
    in_specs = (P("batch", None), P(("proto", "batch"), None))
    out_specs = P("batch", "proto")
    return jax.shard_map(local, mesh=mesh, in_specs=in_specs, out_specs=out_specs, check_vma=False)
```

```python
import functools

import jax
import jax.numpy as jnp
from jax import lax
from jax.experimental import pallas as pl
from jax.experimental.pallas import tpu as pltpu
from jax.sharding import PartitionSpec as P

ITERS = 3
MOST_PARTNERS = 8
BLOCK_BYTES = 20 * 2**20
VMEM = pltpu.VMEM
IN_VMEM = pl.BlockSpec(memory_space=pltpu.VMEM)
F32 = jnp.float32
LANES = 128


def unit_rows(matrix):
    values = matrix.astype(F32)
    scale = lax.rsqrt(1e-06 + jnp.sum(values * values, axis=1, keepdims=True))
    return (values * scale).astype(jnp.bfloat16)


def partners(size, stride, count, step):
    pairs = []
    for index in range(size):
        place = index // stride % count
        other = place ^ step if count & (count - 1) == 0 else (place + step) % count
        pairs.append((index, index + (other - place) * stride))
    return pairs


def from_others(value, axis, stride, count):
    size = lax.axis_size(axis)
    return [lax.ppermute(value, axis, partners(size, stride, count, step)) for step in range(1, count)]


def swap_cores(value):
    return lax.ppermute(value, "proto", partners(lax.axis_size("proto"), 1, 2, 1))


def group_sum(value, axis, stride, count):
    total = value
    for other in from_others(value, axis, stride, count):
        total = total + other
    return total


def proto_sums(partial_value):
    size = lax.axis_size("batch")
    if size > MOST_PARTNERS:
        return lax.psum(partial_value, "batch")
    return group_sum(partial_value, "batch", 1, size)


def image_sums(partial_value):
    size = lax.axis_size("proto")
    if size > 2 * MOST_PARTNERS or size % 2:
        return lax.psum(partial_value, "proto")
    pair = group_sum(partial_value, "proto", 1, 2)
    return group_sum(pair, "proto", 2, size // 2)


def split_plan(features, prototypes):
    unit_feat = unit_rows(features)
    gathered = lax.all_gather(unit_rows(prototypes), "batch", axis=0, tiled=True)
    scores = jnp.einsum("bd,kd->bk", unit_feat, gathered, preferred_element_type=F32)
    weights = jnp.exp(20.0 * scores)
    total_protos = float(weights.shape[1] * lax.axis_size("proto"))
    row_factor = jnp.ones((weights.shape[0],), F32)
    col_factor = jnp.ones((weights.shape[1],), F32)
    for step in range(ITERS):
        column_part = jnp.dot(row_factor, weights, precision=lax.Precision.HIGHEST)
        col_factor = 1.0 / proto_sums(column_part)
        row_part = jnp.dot(weights, col_factor, precision=lax.Precision.HIGHEST)
        row_factor = 1.0 / image_sums(row_part)
    scaled = weights * row_factor[:, None] * (total_protos * col_factor)[None, :]
    return scaled.astype(jnp.bfloat16)


def call(kernel, outs, args, limit, cost=0, aliases=None, scratch=()):
    pinned = [pltpu.with_memory_space_constraint(arg, VMEM) for arg in args]
    return pl.pallas_call(
        kernel,
        out_shape=[VMEM(shape, dtype) for shape, dtype in outs],
        in_specs=[IN_VMEM] * len(pinned),
        out_specs=[IN_VMEM] * len(outs),
        input_output_aliases=aliases or {},
        scratch_shapes=list(scratch),
        compiler_params=pltpu.CompilerParams(vmem_limit_bytes=limit * 2**20),
        cost_estimate=pl.CostEstimate(flops=max(cost,1), bytes_accessed=1, transcendentals=1),
    )(*pinned)


def scores_of(protos, images):
    return lax.dot_general(protos, images, (((1,), (1,)), ((), ())), preferred_element_type=F32)


def tiles(width):
    return [slice(start, start + LANES) for start in range(0, width, LANES)]


def fill(weights, total, rows, columns, unit_proto, unit_feat):
    step = 2 * LANES
    for column in range(columns.start, columns.stop, step):
        values = jnp.exp(20.0 * scores_of(unit_proto, unit_feat[column : column + step, :]))
        weights[rows, column : column + step] = values
        for tile in tiles(step):
            total = total + values[:, tile]
    return total


def add_images(part, weights, rows, col_factor):
    count = col_factor.shape[0]
    for tile in tiles(part.shape[1]):
        product = weights[rows, tile] * col_factor
        part[:, tile] = part[:, tile] + jnp.sum(product.reshape(count // 8, 8, LANES), axis=0)


def spread(lane_sums):
    return jnp.broadcast_to(1.0 / jnp.sum(lane_sums, axis=1, keepdims=True), lane_sums.shape)


def unit_kernel(feats, protos, unit_feat, unit_proto, raw, sems):
    copies = [pltpu.make_async_copy(src, raw.at[i], sems.at[i]) for i, src in enumerate((feats, protos))]
    for copy in copies:
        copy.start()
    for index, unit in enumerate((unit_feat, unit_proto)):
        copies[index].wait()
        unit[...] = unit_rows(raw[index])


def near_kernel(own_feat, near, near_swapped, own_proto, first, unit_feat, unit_proto, weights, sums):
    block = own_feat.shape[0]
    core = lax.axis_index("proto") % 2
    unit_feat[:block, :] = own_feat[...]
    unit_feat[pl.ds(pl.multiple_of((1 + core) * block, block), block), :] = unit_rows(near[...])
    unit_feat[pl.ds(pl.multiple_of((2 - core) * block, block), block), :] = unit_rows(near_swapped[...])
    unit_proto[:block, :] = own_proto[...]
    unit_proto[block : 2 * block, :] = first[...]

    def body(index, carry):
        rows = pl.ds(pl.multiple_of(index * block, block), block)
        total = jnp.zeros((block, LANES), F32)
        sums[rows, :] = fill(weights, total, rows, slice(0, 3 * block), unit_proto[rows, :], unit_feat)
        return carry

    lax.fori_loop(0, 2, body, 0)


def far_kernel(far, far_swapped, sums, unit_proto, feat_in, weights_in, unit_feat, weights, part):
    half = far.shape[0]
    block = 2 * half
    core = lax.axis_index("proto") % 2
    unit_feat[pl.ds(pl.multiple_of(3 * block + (1 - core) * half, half), half), :] = unit_rows(far[...])
    unit_feat[pl.ds(pl.multiple_of(3 * block + core * half, half), half), :] = unit_rows(far_swapped[...])
    part[...] = jnp.zeros(part.shape, F32)

    def body(index, carry):
        rows = pl.ds(pl.multiple_of(index * block, block), block)
        total = fill(weights, sums[rows, :], rows, slice(3 * block, 4 * block), unit_proto[rows, :], unit_feat)
        add_images(part, weights, rows, spread(total))
        return carry

    lax.fori_loop(0, 2, body, 0)


def more_kernel(start, ready,  unit_feat, proto_in, weights_in, part_in, unit_proto, weights, part, *row_sums):
    rows = slice(start, start + ready.shape[0])
    unit_proto[rows, :] = ready[...]
    total = jnp.zeros((ready.shape[0], LANES), F32)
    total = fill(weights, total, rows, slice(0, weights.shape[1]), unit_proto[rows, :], unit_feat)
    add_images(part, weights, rows, spread(total))
    for store in row_sums:
        store[...] = flat(part)


def flat(part):
    return jnp.sum(part[...], axis=0, keepdims=True)


def summed(parts):
    total = parts[0][...]
    for part in parts[1:]:
        total = total + part[...]
    return total


def pass_kernel(count, block, *refs):
    parts, weights, row_sums, *col_factor, part = refs[:count], *refs[count:]
    row_factor = 1.0 / summed(parts)
    part[...] = jnp.zeros(part.shape, F32)

    def body(index, carry):
        rows = pl.ds(pl.multiple_of(index * block, block), block)
        total = jnp.zeros((block, LANES), F32)
        for tile in tiles(weights.shape[1]):
            total = total + weights[rows, tile] * row_factor[:, tile]
        factor = spread(total)
        for store in col_factor:
            store[rows, :] = factor
        add_images(part, weights, rows, factor)
        return carry

    lax.fori_loop(0, weights.shape[0] // block, body, 0)
    row_sums[...] = flat(part)


def ready_kernel(scale, unit_feat, unit_proto, col_factor, ready):
    block = ready.shape[0]
    images = unit_feat[:block, :]
    for start in range(0, ready.shape[1], block):
        values = jnp.exp(20.0 * scores_of(images, unit_proto[start : start + block, :]))
        for tile in tiles(block):
            at = slice(start + tile.start, start + tile.stop)
            factor = scale * jnp.transpose(col_factor[at, :])[:1, :]
            ready[:, at] = values[:, tile] * factor


def last_kernel(count, block, *refs):
    parts, ready, out, staged, sems = refs[:count], *refs[count:]
    total = summed(parts)
    factors = []
    for tile in tiles(block):
        factors.append(jnp.transpose(jnp.broadcast_to(1.0 / total[:, tile], (LANES, LANES))))
    factor = jnp.concatenate(factors, axis=0)
    place = lax.axis_index("batch")
    core = lax.axis_index("proto") % 2
    copies = []
    for index, step in enumerate((0, 1 + core, 2 - core, 3)):
        for tile in tiles(block):
            values = ready[:, index * block + tile.start : index * block + tile.stop]
            staged[index, :, tile] = (values * factor).astype(staged.dtype)
        column = pl.multiple_of(jnp.bitwise_xor(place, step) * block, block)
        copies.append(pltpu.make_async_copy(staged.at[index], out.at[:, pl.ds(column, block)], sems.at[index]))
        copies[-1].start()
    for copy in copies:
        copy.wait()


def by_core(steps):
    protos, blocks = lax.axis_size("proto"), lax.axis_size("batch")
    return [
        (place * protos + proto, (place ^ steps[proto % 2]) * protos + proto)
        for place in range(blocks)
        for proto in range(protos)
    ]


def send(value, steps):
    return lax.ppermute(value, ("batch", "proto"), by_core(steps))


def whole_plan(features, prototypes):
    bf16 = jnp.bfloat16
    blocks = lax.axis_size("batch")
    block, depth = features.shape
    images = blocks * block
    z_count = lax.axis_size("proto") // 2
    total_protos = float(images * lax.axis_size("proto"))
    feat_shape = ((images, depth), bf16)
    weights_shape = ((images, images), F32)
    part_shape = ((8, images), F32)
    lanes_shape = ((images, LANES), F32)

    half = block // 2
    core = lax.axis_index("proto") % 2
    own_feat, own_proto = pl.pallas_call(
        unit_kernel,
        out_shape=[VMEM((block, depth), bf16)] * 2,
        in_specs=[pl.BlockSpec(memory_space=pltpu.HBM)] * 2,
        out_specs=[IN_VMEM] * 2,
        scratch_shapes=[VMEM((2, block, depth), bf16), pltpu.SemaphoreType.DMA((2,))],
        compiler_params=pltpu.CompilerParams(vmem_limit_bytes=4 * 2**20),
        cost_estimate=pl.CostEstimate(flops=1, bytes_accessed=1, transcendentals=1),
    )(*[pltpu.with_memory_space_constraint(arg, pltpu.HBM) for arg in (features, prototypes)])
    near = send(features, (1, 2))
    first = send(own_proto, (1, 2))
    second = send(own_proto, (2, 1))
    near_half = lax.dynamic_slice_in_dim(near, (1 - core) * half, half, 0)
    forward, own_feat, own_proto = lax.optimization_barrier((near_half, own_feat, own_proto))
    far = send(forward, (2, 1))
    cut = 3 * block // 4
    last = [send(first[:cut], (2, 1)), send(first[cut:], (2, 1))]
    unit_feat, unit_proto, weights, sums = call(
        near_kernel,
        [feat_shape, feat_shape, weights_shape, lanes_shape],
        [own_feat, near, swap_cores(near), own_proto, first],
        16,
    )
    far, sums = lax.optimization_barrier((far, sums))
    unit_feat, weights, part = call(
        far_kernel,
        [feat_shape, weights_shape, part_shape],
        [far, swap_cores(far), sums, unit_proto, unit_feat, weights],
        16,
        aliases={4: 0, 5: 1},
    )
    outs = [feat_shape, weights_shape, part_shape, ((1, images), F32)]
    start = 2 * block
    for piece in (second, *last):
        end = start + piece.shape[0]
        unit_proto, weights, part, *row_sums = call(
            functools.partial(more_kernel, start),
            outs if end == images else outs[:3],
            [piece, unit_feat, unit_proto, weights, part],
            16,
            aliases={2: 0, 3: 1, 4: 2},
        )
        start = end

    def around(value):
        total = value + swap_cores(value)
        others = from_others(total, "proto", 2, z_count)
        order = (2, 1, 3) if value.shape[1] < images else (3, 2, 1)
        for k in order:
            total = lax.optimization_barrier(total + others[k - 1])
        return [total]

    parts = around(*row_sums)
    for step in range(1, ITERS):
        final = step == ITERS - 1
        wanted = block if final else images
        row_sums, *col_factor = call(
            functools.partial(pass_kernel, len(parts), block),
            [((1, wanted), F32), lanes_shape] if final else [((1, wanted), F32)],
            [*parts, weights],
            8,
            cost=4 * images * images,
            scratch=[VMEM((8, wanted), F32)],
        )
        parts = around(row_sums)
    (ready,) = call(
        functools.partial(ready_kernel, total_protos),
        [((block, images), F32)],
        [unit_feat, unit_proto, *col_factor],
        16,
        cost=2 * block * images * depth,
    )
    pinned = [pltpu.with_memory_space_constraint(arg, VMEM) for arg in [*parts, ready]]
    return pl.pallas_call(
        functools.partial(last_kernel, len(parts), block),
        out_shape=jax.ShapeDtypeStruct((block, images), bf16),
        in_specs=[IN_VMEM] * len(pinned),
        out_specs=pl.BlockSpec(memory_space=pl.ANY),
        scratch_shapes=[VMEM((blocks, block, block), bf16), pltpu.SemaphoreType.DMA((blocks,))],
        compiler_params=pltpu.CompilerParams(vmem_limit_bytes=8 * 2**20),
    )(*pinned)


def local(features, prototypes):
    blocks = lax.axis_size("batch")
    block, height = features.shape[0], prototypes.shape[0]
    fits = 4 * blocks * blocks * block * height <= BLOCK_BYTES
    even = block == height and block % (2 * LANES) == 0 and blocks == 4
    if fits and even and lax.axis_size("proto") % 2 == 0 and lax.axis_size("proto") <= 2 * MOST_PARTNERS:
        return whole_plan(features, prototypes)
    return split_plan(features, prototypes)


def solution(mesh):
    in_specs = (P("batch", None), P(("proto", "batch"), None))
    out_specs = P("batch", "proto")
    return jax.shard_map(local, mesh=mesh, in_specs=in_specs, out_specs=out_specs, check_vma=False)
```

```python
import functools

import jax
import jax.numpy as jnp
from jax import lax
from jax.experimental import pallas as pl
from jax.experimental.pallas import tpu as pltpu
from jax.sharding import PartitionSpec as P

ITERS = 3
MOST_PARTNERS = 8
BLOCK_BYTES = 20 * 2**20
VMEM = pltpu.VMEM
IN_VMEM = pl.BlockSpec(memory_space=pltpu.VMEM)
F32 = jnp.float32
LANES = 128


def unit_rows(matrix):
    values = matrix.astype(F32)
    scale = lax.rsqrt(1e-06 + jnp.sum(values * values, axis=1, keepdims=True))
    return (values * scale).astype(jnp.bfloat16)


def partners(size, stride, count, step):
    pairs = []
    for index in range(size):
        place = index // stride % count
        other = place ^ step if count & (count - 1) == 0 else (place + step) % count
        pairs.append((index, index + (other - place) * stride))
    return pairs


def from_others(value, axis, stride, count):
    size = lax.axis_size(axis)
    return [lax.ppermute(value, axis, partners(size, stride, count, step)) for step in range(1, count)]


def swap_cores(value):
    return lax.ppermute(value, "proto", partners(lax.axis_size("proto"), 1, 2, 1))


def group_sum(value, axis, stride, count):
    total = value
    for other in from_others(value, axis, stride, count):
        total = total + other
    return total


def proto_sums(partial_value):
    size = lax.axis_size("batch")
    if size > MOST_PARTNERS:
        return lax.psum(partial_value, "batch")
    return group_sum(partial_value, "batch", 1, size)


def image_sums(partial_value):
    size = lax.axis_size("proto")
    if size > 2 * MOST_PARTNERS or size % 2:
        return lax.psum(partial_value, "proto")
    pair = group_sum(partial_value, "proto", 1, 2)
    return group_sum(pair, "proto", 2, size // 2)


def split_plan(features, prototypes):
    unit_feat = unit_rows(features)
    gathered = lax.all_gather(unit_rows(prototypes), "batch", axis=0, tiled=True)
    scores = jnp.einsum("bd,kd->bk", unit_feat, gathered, preferred_element_type=F32)
    weights = jnp.exp(20.0 * scores)
    total_protos = float(weights.shape[1] * lax.axis_size("proto"))
    row_factor = jnp.ones((weights.shape[0],), F32)
    col_factor = jnp.ones((weights.shape[1],), F32)
    for step in range(ITERS):
        column_part = jnp.dot(row_factor, weights, precision=lax.Precision.HIGHEST)
        col_factor = 1.0 / proto_sums(column_part)
        row_part = jnp.dot(weights, col_factor, precision=lax.Precision.HIGHEST)
        row_factor = 1.0 / image_sums(row_part)
    scaled = weights * row_factor[:, None] * (total_protos * col_factor)[None, :]
    return scaled.astype(jnp.bfloat16)


def call(kernel, outs, args, limit, cost=0, aliases=None, scratch=()):
    pinned = [pltpu.with_memory_space_constraint(arg, VMEM) for arg in args]
    return pl.pallas_call(
        kernel,
        out_shape=[VMEM(shape, dtype) for shape, dtype in outs],
        in_specs=[IN_VMEM] * len(pinned),
        out_specs=[IN_VMEM] * len(outs),
        input_output_aliases=aliases or {},
        scratch_shapes=list(scratch),
        compiler_params=pltpu.CompilerParams(vmem_limit_bytes=limit * 2**20),
        cost_estimate=pl.CostEstimate(flops=max(cost,1), bytes_accessed=1, transcendentals=1),
    )(*pinned)


def scores_of(protos, images):
    return lax.dot_general(protos, images, (((1,), (1,)), ((), ())), preferred_element_type=F32)


def tiles(width):
    return [slice(start, start + LANES) for start in range(0, width, LANES)]


def fill(weights, total, rows, columns, unit_proto, unit_feat):
    step = 2 * LANES
    for column in range(columns.start, columns.stop, step):
        values = jnp.exp(20.0 * scores_of(unit_proto, unit_feat[column : column + step, :]))
        weights[rows, column : column + step] = values
        for tile in tiles(step):
            total = total + values[:, tile]
    return total


def add_images(part, weights, rows, col_factor):
    count = col_factor.shape[0]
    for tile in tiles(part.shape[1]):
        product = weights[rows, tile] * col_factor
        part[:, tile] = part[:, tile] + jnp.sum(product.reshape(count // 8, 8, LANES), axis=0)


def spread(lane_sums):
    return jnp.broadcast_to(1.0 / jnp.sum(lane_sums, axis=1, keepdims=True), lane_sums.shape)


def unit_kernel(feats, protos, unit_feat, unit_proto, raw, sems):
    copies = [pltpu.make_async_copy(src, raw.at[i], sems.at[i]) for i, src in enumerate((feats, protos))]
    for copy in copies:
        copy.start()
    for index, unit in enumerate((unit_feat, unit_proto)):
        copies[index].wait()
        unit[...] = unit_rows(raw[index])


def near_kernel(own_feat, near, near_swapped, own_proto, unit_feat, unit_proto, weights, sums):
    block = own_feat.shape[0]
    core = lax.axis_index("proto") % 2
    unit_feat[:block, :] = own_feat[...]
    unit_feat[pl.ds(pl.multiple_of((1 + core) * block, block), block), :] = unit_rows(near[...])
    unit_feat[pl.ds(pl.multiple_of((2 - core) * block, block), block), :] = unit_rows(near_swapped[...])
    unit_proto[:block, :] = own_proto[...]
    total = jnp.zeros((block, LANES), F32)
    sums[:block, :] = fill(weights, total, slice(0, block), slice(0, 3 * block), own_proto[...], unit_feat)


def first_kernel(first, sums_in, unit_feat, proto_in, weights_in, sums, unit_proto, weights):
    block = first.shape[0]
    rows = slice(block, 2 * block)
    unit_proto[rows, :] = first[...]
    total = jnp.zeros((block, LANES), F32)
    sums[rows, :] = fill(weights, total, rows, slice(0, 3 * block), first[...], unit_feat)


def far_kernel(far, far_swapped, sums, unit_proto, feat_in, weights_in, unit_feat, weights, part):
    half = far.shape[0]
    block = 2 * half
    core = lax.axis_index("proto") % 2
    unit_feat[pl.ds(pl.multiple_of(3 * block + (1 - core) * half, half), half), :] = unit_rows(far[...])
    unit_feat[pl.ds(pl.multiple_of(3 * block + core * half, half), half), :] = unit_rows(far_swapped[...])
    part[...] = jnp.zeros(part.shape, F32)

    def body(index, carry):
        rows = pl.ds(pl.multiple_of(index * block, block), block)
        total = fill(weights, sums[rows, :], rows, slice(3 * block, 4 * block), unit_proto[rows, :], unit_feat)
        add_images(part, weights, rows, spread(total))
        return carry

    lax.fori_loop(0, 2, body, 0)


def more_kernel(start, ready,  unit_feat, proto_in, weights_in, part_in, unit_proto, weights, part, *row_sums):
    rows = slice(start, start + ready.shape[0])
    unit_proto[rows, :] = ready[...]
    total = jnp.zeros((ready.shape[0], LANES), F32)
    total = fill(weights, total, rows, slice(0, weights.shape[1]), unit_proto[rows, :], unit_feat)
    add_images(part, weights, rows, spread(total))
    for store in row_sums:
        store[...] = flat(part)


def flat(part):
    return jnp.sum(part[...], axis=0, keepdims=True)


def summed(parts):
    total = parts[0][...]
    for part in parts[1:]:
        total = total + part[...]
    return total


def pass_kernel(count, block, *refs):
    parts, weights, row_sums, *col_factor, part = refs[:count], *refs[count:]
    row_factor = 1.0 / summed(parts)
    part[...] = jnp.zeros(part.shape, F32)

    def body(index, carry):
        rows = pl.ds(pl.multiple_of(index * block, block), block)
        total = jnp.zeros((block, LANES), F32)
        for tile in tiles(weights.shape[1]):
            total = total + weights[rows, tile] * row_factor[:, tile]
        factor = spread(total)
        for store in col_factor:
            store[rows, :] = factor
        add_images(part, weights, rows, factor)
        return carry

    lax.fori_loop(0, weights.shape[0] // block, body, 0)
    row_sums[...] = flat(part)


def ready_kernel(scale, unit_feat, unit_proto, col_factor, ready):
    block = ready.shape[0]
    images = unit_feat[:block, :]
    for start in range(0, ready.shape[1], block):
        values = jnp.exp(20.0 * scores_of(images, unit_proto[start : start + block, :]))
        for tile in tiles(block):
            at = slice(start + tile.start, start + tile.stop)
            factor = scale * jnp.transpose(col_factor[at, :])[:1, :]
            ready[:, at] = values[:, tile] * factor


def last_kernel(count, block, *refs):
    parts, ready, out, staged, sems = refs[:count], *refs[count:]
    inverse = 1.0 / summed(parts)
    place = lax.axis_index("batch")
    core = lax.axis_index("proto") % 2
    bases = [jnp.bitwise_xor(place, step) * block for step in (0, 1 + core, 2 - core, 3)]
    height = block // sems.shape[0]
    copies = []
    for index in range(sems.shape[0]):
        rows = slice(index * height, (index + 1) * height)
        group = rows.start // LANES * LANES
        spread_rows = jnp.transpose(jnp.broadcast_to(inverse[:, group : group + LANES], (LANES, LANES)))
        factor = spread_rows[rows.start - group : rows.stop - group]
        for number, base in enumerate(bases):
            for tile in tiles(block):
                values = ready[rows, number * block + tile.start : number * block + tile.stop]
                column = pl.multiple_of(base + tile.start, LANES)
                staged[rows, pl.ds(column, LANES)] = (values * factor).astype(staged.dtype)
        copies.append(pltpu.make_async_copy(staged.at[rows], out.at[rows], sems.at[index]))
        copies[-1].start()
    for copy in copies:
        copy.wait()


def by_core(steps):
    protos, blocks = lax.axis_size("proto"), lax.axis_size("batch")
    return [
        (place * protos + proto, (place ^ steps[proto % 2]) * protos + proto)
        for place in range(blocks)
        for proto in range(protos)
    ]


def send(value, steps):
    return lax.ppermute(value, ("batch", "proto"), by_core(steps))


def whole_plan(features, prototypes):
    bf16 = jnp.bfloat16
    blocks = lax.axis_size("batch")
    block, depth = features.shape
    images = blocks * block
    z_count = lax.axis_size("proto") // 2
    total_protos = float(images * lax.axis_size("proto"))
    feat_shape = ((images, depth), bf16)
    weights_shape = ((images, images), F32)
    part_shape = ((8, images), F32)
    lanes_shape = ((images, LANES), F32)

    half = block // 2
    core = lax.axis_index("proto") % 2
    own_feat, own_proto = pl.pallas_call(
        unit_kernel,
        out_shape=[VMEM((block, depth), bf16)] * 2,
        in_specs=[pl.BlockSpec(memory_space=pltpu.HBM)] * 2,
        out_specs=[IN_VMEM] * 2,
        scratch_shapes=[VMEM((2, block, depth), bf16), pltpu.SemaphoreType.DMA((2,))],
        compiler_params=pltpu.CompilerParams(vmem_limit_bytes=4 * 2**20),
        cost_estimate=pl.CostEstimate(flops=1, bytes_accessed=1, transcendentals=1),
    )(*[pltpu.with_memory_space_constraint(arg, pltpu.HBM) for arg in (features, prototypes)])
    near = send(features, (1, 2))
    first = send(own_proto, (1, 2))
    second = send(own_proto, (2, 1))
    near_half = lax.dynamic_slice_in_dim(near, (1 - core) * half, half, 0)
    forward, own_feat, own_proto = lax.optimization_barrier((near_half, own_feat, own_proto))
    far = send(forward, (2, 1))
    unit_feat, unit_proto, weights, sums = call(
        near_kernel,
        [feat_shape, feat_shape, weights_shape, lanes_shape],
        [own_feat, near, swap_cores(near), own_proto],
        16,
    )
    far, sums = lax.optimization_barrier((far, sums))
    cut = 5 * block // 8
    last = [send(first[:cut], (2, 1)), send(first[cut:], (2, 1))]
    sums, unit_proto, weights = call(
        first_kernel,
        [lanes_shape, feat_shape, weights_shape],
        [first, sums, unit_feat, unit_proto, weights],
        16,
        aliases={1: 0, 3: 1, 4: 2},
    )
    unit_feat, weights, part = call(
        far_kernel,
        [feat_shape, weights_shape, part_shape],
        [far, swap_cores(far), sums, unit_proto, unit_feat, weights],
        16,
        aliases={4: 0, 5: 1},
    )
    outs = [feat_shape, weights_shape, part_shape, ((1, images), F32)]
    start = 2 * block
    for piece in (second, *last):
        end = start + piece.shape[0]
        unit_proto, weights, part, *row_sums = call(
            functools.partial(more_kernel, start),
            outs if end == images else outs[:3],
            [piece, unit_feat, unit_proto, weights, part],
            16,
            aliases={2: 0, 3: 1, 4: 2},
        )
        start = end

    def around(value):
        total = value + swap_cores(value)
        for other in reversed(from_others(total, "proto", 2, z_count)):
            total = lax.optimization_barrier(total + other)
        return [total]

    parts = around(*row_sums)
    for step in range(1, ITERS):
        final = step == ITERS - 1
        wanted = block if final else images
        row_sums, *col_factor = call(
            functools.partial(pass_kernel, len(parts), block),
            [((1, wanted), F32), lanes_shape] if final else [((1, wanted), F32)],
            [*parts, weights],
            8,
            cost=4 * images * images,
            scratch=[VMEM((8, wanted), F32)],
        )
        parts = around(row_sums)
    (ready,) = call(
        functools.partial(ready_kernel, total_protos),
        [((block, images), F32)],
        [unit_feat, unit_proto, *col_factor],
        16,
        cost=2 * block * images * depth,
    )
    pinned = [pltpu.with_memory_space_constraint(arg, VMEM) for arg in [*parts, ready]]
    return pl.pallas_call(
        functools.partial(last_kernel, len(parts), block),
        out_shape=jax.ShapeDtypeStruct((block, images), bf16),
        in_specs=[IN_VMEM] * len(pinned),
        out_specs=pl.BlockSpec(memory_space=pl.ANY),
        scratch_shapes=[VMEM((block, images), bf16), pltpu.SemaphoreType.DMA((2 * block // LANES,))],
        compiler_params=pltpu.CompilerParams(vmem_limit_bytes=8 * 2**20),
    )(*pinned)


def local(features, prototypes):
    blocks = lax.axis_size("batch")
    block, height = features.shape[0], prototypes.shape[0]
    fits = 4 * blocks * blocks * block * height <= BLOCK_BYTES
    even = block == height and block % (2 * LANES) == 0 and blocks == 4
    if fits and even and lax.axis_size("proto") % 2 == 0 and lax.axis_size("proto") <= 2 * MOST_PARTNERS:
        return whole_plan(features, prototypes)
    return split_plan(features, prototypes)


def solution(mesh):
    in_specs = (P("batch", None), P(("proto", "batch"), None))
    out_specs = P("batch", "proto")
    return jax.shard_map(local, mesh=mesh, in_specs=in_specs, out_specs=out_specs, check_vma=False)
```

```python
import functools

import jax
import jax.numpy as jnp
from jax import lax
from jax.experimental import pallas as pl
from jax.experimental.pallas import tpu as pltpu
from jax.sharding import PartitionSpec as P

ITERS = 3
MOST_PARTNERS = 8
BLOCK_BYTES = 20 * 2**20
VMEM = pltpu.VMEM
IN_VMEM = pl.BlockSpec(memory_space=pltpu.VMEM)
F32 = jnp.float32
LANES = 128


def unit_rows(matrix):
    values = matrix.astype(F32)
    scale = lax.rsqrt(1e-06 + jnp.sum(values * values, axis=1, keepdims=True))
    return (values * scale).astype(jnp.bfloat16)


def partners(size, stride, count, step):
    pairs = []
    for index in range(size):
        place = index // stride % count
        other = place ^ step if count & (count - 1) == 0 else (place + step) % count
        pairs.append((index, index + (other - place) * stride))
    return pairs


def from_others(value, axis, stride, count):
    size = lax.axis_size(axis)
    return [lax.ppermute(value, axis, partners(size, stride, count, step)) for step in range(1, count)]


def swap_cores(value):
    return lax.ppermute(value, "proto", partners(lax.axis_size("proto"), 1, 2, 1))


def group_sum(value, axis, stride, count):
    total = value
    for other in from_others(value, axis, stride, count):
        total = total + other
    return total


def proto_sums(partial_value):
    size = lax.axis_size("batch")
    if size > MOST_PARTNERS:
        return lax.psum(partial_value, "batch")
    return group_sum(partial_value, "batch", 1, size)


def image_sums(partial_value):
    size = lax.axis_size("proto")
    if size > 2 * MOST_PARTNERS or size % 2:
        return lax.psum(partial_value, "proto")
    pair = group_sum(partial_value, "proto", 1, 2)
    return group_sum(pair, "proto", 2, size // 2)


def split_plan(features, prototypes):
    unit_feat = unit_rows(features)
    gathered = lax.all_gather(unit_rows(prototypes), "batch", axis=0, tiled=True)
    scores = jnp.einsum("bd,kd->bk", unit_feat, gathered, preferred_element_type=F32)
    weights = jnp.exp(20.0 * scores)
    total_protos = float(weights.shape[1] * lax.axis_size("proto"))
    row_factor = jnp.ones((weights.shape[0],), F32)
    col_factor = jnp.ones((weights.shape[1],), F32)
    for step in range(ITERS):
        column_part = jnp.dot(row_factor, weights, precision=lax.Precision.HIGHEST)
        col_factor = 1.0 / proto_sums(column_part)
        row_part = jnp.dot(weights, col_factor, precision=lax.Precision.HIGHEST)
        row_factor = 1.0 / image_sums(row_part)
    scaled = weights * row_factor[:, None] * (total_protos * col_factor)[None, :]
    return scaled.astype(jnp.bfloat16)


def call(kernel, outs, args, limit, cost=0, aliases=None, scratch=()):
    pinned = [pltpu.with_memory_space_constraint(arg, VMEM) for arg in args]
    return pl.pallas_call(
        kernel,
        out_shape=[VMEM(shape, dtype) for shape, dtype in outs],
        in_specs=[IN_VMEM] * len(pinned),
        out_specs=[IN_VMEM] * len(outs),
        input_output_aliases=aliases or {},
        scratch_shapes=list(scratch),
        compiler_params=pltpu.CompilerParams(vmem_limit_bytes=limit * 2**20),
        cost_estimate=pl.CostEstimate(flops=max(cost,1), bytes_accessed=1, transcendentals=1),
    )(*pinned)


def scores_of(protos, images):
    return lax.dot_general(protos, images, (((1,), (1,)), ((), ())), preferred_element_type=F32)


def tiles(width):
    return [slice(start, start + LANES) for start in range(0, width, LANES)]


def fill(weights, total, rows, columns, unit_proto, unit_feat):
    step = 2 * LANES
    for column in range(columns.start, columns.stop, step):
        values = jnp.exp(20.0 * scores_of(unit_proto, unit_feat[column : column + step, :]))
        weights[rows, column : column + step] = values
        for tile in tiles(step):
            total = total + values[:, tile]
    return total


def add_images(part, weights, rows, col_factor):
    count = col_factor.shape[0]
    for tile in tiles(part.shape[1]):
        product = weights[rows, tile] * col_factor
        part[:, tile] = part[:, tile] + jnp.sum(product.reshape(count // 8, 8, LANES), axis=0)


def spread(lane_sums):
    return jnp.broadcast_to(1.0 / jnp.sum(lane_sums, axis=1, keepdims=True), lane_sums.shape)


def unit_kernel(feats, protos, unit_feat, unit_proto, raw, sems):
    copies = [pltpu.make_async_copy(src, raw.at[i], sems.at[i]) for i, src in enumerate((feats, protos))]
    for copy in copies:
        copy.start()
    for index, unit in enumerate((unit_feat, unit_proto)):
        copies[index].wait()
        unit[...] = unit_rows(raw[index])


def near_kernel(own_feat, near, near_swapped, own_proto, unit_feat, unit_proto, weights, sums):
    block = own_feat.shape[0]
    core = lax.axis_index("proto") % 2
    unit_feat[:block, :] = own_feat[...]
    unit_feat[pl.ds(pl.multiple_of((1 + core) * block, block), block), :] = unit_rows(near[...])
    unit_feat[pl.ds(pl.multiple_of((2 - core) * block, block), block), :] = unit_rows(near_swapped[...])
    unit_proto[:block, :] = own_proto[...]
    total = jnp.zeros((block, LANES), F32)
    sums[:block, :] = fill(weights, total, slice(0, block), slice(0, 3 * block), own_proto[...], unit_feat)


def first_kernel(first, sums_in, unit_feat, proto_in, weights_in, sums, unit_proto, weights):
    block = first.shape[0]
    rows = slice(block, 2 * block)
    unit_proto[rows, :] = first[...]
    total = jnp.zeros((block, LANES), F32)
    sums[rows, :] = fill(weights, total, rows, slice(0, 3 * block), first[...], unit_feat)


def far_kernel(far, *refs):
    *far_swapped, sums, unit_proto, feat_in, weights_in, unit_feat, weights, part = refs
    half = far.shape[0]
    block = 2 * half
    core = lax.axis_index("proto") % 2
    unit_feat[pl.ds(pl.multiple_of(3 * block + (1 - core) * half, half), half), :] = unit_rows(far[...])
    height = half // len(far_swapped)
    for index, piece in enumerate(far_swapped):
        start = pl.multiple_of(3 * block + core * half + index * height, height)
        unit_feat[pl.ds(start, height), :] = unit_rows(piece[...])
    part[...] = jnp.zeros(part.shape, F32)

    def body(index, carry):
        rows = pl.ds(pl.multiple_of(index * block, block), block)
        total = fill(weights, sums[rows, :], rows, slice(3 * block, 4 * block), unit_proto[rows, :], unit_feat)
        add_images(part, weights, rows, spread(total))
        return carry

    lax.fori_loop(0, 2, body, 0)


def more_kernel(start, ready,  unit_feat, proto_in, weights_in, part_in, unit_proto, weights, part, *row_sums):
    rows = slice(start, start + ready.shape[0])
    unit_proto[rows, :] = ready[...]
    total = jnp.zeros((ready.shape[0], LANES), F32)
    total = fill(weights, total, rows, slice(0, weights.shape[1]), unit_proto[rows, :], unit_feat)
    add_images(part, weights, rows, spread(total))
    for store in row_sums:
        store[...] = flat(part)


def flat(part):
    return jnp.sum(part[...], axis=0, keepdims=True)


def summed(parts):
    total = parts[0][...]
    for part in parts[1:]:
        total = total + part[...]
    return total


def pass_kernel(count, block, *refs):
    parts, weights, row_sums, *col_factor, part = refs[:count], *refs[count:]
    row_factor = 1.0 / summed(parts)
    part[...] = jnp.zeros(part.shape, F32)

    def body(index, carry):
        rows = pl.ds(pl.multiple_of(index * block, block), block)
        total = jnp.zeros((block, LANES), F32)
        for tile in tiles(weights.shape[1]):
            total = total + weights[rows, tile] * row_factor[:, tile]
        factor = spread(total)
        for store in col_factor:
            store[rows, :] = factor
        add_images(part, weights, rows, factor)
        return carry

    lax.fori_loop(0, weights.shape[0] // block, body, 0)
    row_sums[...] = flat(part)


def ready_kernel(scale, unit_feat, unit_proto, col_factor, ready):
    block = ready.shape[0]
    images = unit_feat[:block, :]
    for start in range(0, ready.shape[1], block):
        values = jnp.exp(20.0 * scores_of(images, unit_proto[start : start + block, :]))
        for tile in tiles(block):
            at = slice(start + tile.start, start + tile.stop)
            factor = scale * jnp.transpose(col_factor[at, :])[:1, :]
            ready[:, at] = values[:, tile] * factor


def last_kernel(count, block, *refs):
    parts, ready, out, staged, sems = refs[:count], *refs[count:]
    inverse = 1.0 / summed(parts)
    place = lax.axis_index("batch")
    core = lax.axis_index("proto") % 2
    bases = [jnp.bitwise_xor(place, step) * block for step in (0, 1 + core, 2 - core, 3)]
    height = block // sems.shape[0]
    copies = []
    for index in range(sems.shape[0]):
        rows = slice(index * height, (index + 1) * height)
        group = rows.start // LANES * LANES
        spread_rows = jnp.transpose(jnp.broadcast_to(inverse[:, group : group + LANES], (LANES, LANES)))
        factor = spread_rows[rows.start - group : rows.stop - group]
        for number, base in enumerate(bases):
            for tile in tiles(block):
                values = ready[rows, number * block + tile.start : number * block + tile.stop]
                column = pl.multiple_of(base + tile.start, LANES)
                staged[rows, pl.ds(column, LANES)] = (values * factor).astype(staged.dtype)
        copies.append(pltpu.make_async_copy(staged.at[rows], out.at[rows], sems.at[index]))
        copies[-1].start()
    for copy in copies:
        copy.wait()


def by_core(steps):
    protos, blocks = lax.axis_size("proto"), lax.axis_size("batch")
    return [
        (place * protos + proto, (place ^ steps[proto % 2]) * protos + proto)
        for place in range(blocks)
        for proto in range(protos)
    ]


def send(value, steps):
    return lax.ppermute(value, ("batch", "proto"), by_core(steps))


def whole_plan(features, prototypes):
    bf16 = jnp.bfloat16
    blocks = lax.axis_size("batch")
    block, depth = features.shape
    images = blocks * block
    z_count = lax.axis_size("proto") // 2
    total_protos = float(images * lax.axis_size("proto"))
    feat_shape = ((images, depth), bf16)
    weights_shape = ((images, images), F32)
    part_shape = ((8, images), F32)
    lanes_shape = ((images, LANES), F32)

    half = block // 2
    core = lax.axis_index("proto") % 2
    own_feat, own_proto = pl.pallas_call(
        unit_kernel,
        out_shape=[VMEM((block, depth), bf16)] * 2,
        in_specs=[pl.BlockSpec(memory_space=pltpu.HBM)] * 2,
        out_specs=[IN_VMEM] * 2,
        scratch_shapes=[VMEM((2, block, depth), bf16), pltpu.SemaphoreType.DMA((2,))],
        compiler_params=pltpu.CompilerParams(vmem_limit_bytes=4 * 2**20),
        cost_estimate=pl.CostEstimate(flops=1, bytes_accessed=1, transcendentals=1),
    )(*[pltpu.with_memory_space_constraint(arg, pltpu.HBM) for arg in (features, prototypes)])
    near = send(features, (1, 2))
    first = send(own_proto, (1, 2))
    second = send(own_proto, (2, 1))
    near_half = lax.dynamic_slice_in_dim(near, (1 - core) * half, half, 0)
    forward, own_feat, own_proto = lax.optimization_barrier((near_half, own_feat, own_proto))
    far = send(forward, (2, 1))
    unit_feat, unit_proto, weights, sums = call(
        near_kernel,
        [feat_shape, feat_shape, weights_shape, lanes_shape],
        [own_feat, near, swap_cores(near), own_proto],
        16,
    )
    far, sums = lax.optimization_barrier((far, sums))
    cut = 11 * block // 16
    last = [send(first[:cut], (2, 1)), send(first[cut:], (2, 1))]
    sums, unit_proto, weights = call(
        first_kernel,
        [lanes_shape, feat_shape, weights_shape],
        [first, sums, unit_feat, unit_proto, weights],
        16,
        aliases={1: 0, 3: 1, 4: 2},
    )
    swapped = [swap_cores(far[: half // 2]), swap_cores(far[half // 2 :])]
    unit_feat, weights, part = call(
        far_kernel,
        [feat_shape, weights_shape, part_shape],
        [far, *swapped, sums, unit_proto, unit_feat, weights],
        16,
        aliases={3 + len(swapped): 0, 4 + len(swapped): 1},
    )
    outs = [feat_shape, weights_shape, part_shape, ((1, images), F32)]
    start = 2 * block
    for piece in (second, *last):
        end = start + piece.shape[0]
        unit_proto, weights, part, *row_sums = call(
            functools.partial(more_kernel, start),
            outs if end == images else outs[:3],
            [piece, unit_feat, unit_proto, weights, part],
            16,
            aliases={2: 0, 3: 1, 4: 2},
        )
        start = end

    def around(value):
        total = value + swap_cores(value)
        for other in reversed(from_others(total, "proto", 2, z_count)):
            total = lax.optimization_barrier(total + other)
        return [total]

    parts = around(*row_sums)
    for step in range(1, ITERS):
        final = step == ITERS - 1
        wanted = block if final else images
        row_sums, *col_factor = call(
            functools.partial(pass_kernel, len(parts), block),
            [((1, wanted), F32), lanes_shape] if final else [((1, wanted), F32)],
            [*parts, weights],
            8,
            cost=4 * images * images,
            scratch=[VMEM((8, wanted), F32)],
        )
        parts = around(row_sums)
    (ready,) = call(
        functools.partial(ready_kernel, total_protos),
        [((block, images), F32)],
        [unit_feat, unit_proto, *col_factor],
        16,
        cost=2 * block * images * depth,
    )
    pinned = [pltpu.with_memory_space_constraint(arg, VMEM) for arg in [*parts, ready]]
    return pl.pallas_call(
        functools.partial(last_kernel, len(parts), block),
        out_shape=jax.ShapeDtypeStruct((block, images), bf16),
        in_specs=[IN_VMEM] * len(pinned),
        out_specs=pl.BlockSpec(memory_space=pl.ANY),
        scratch_shapes=[VMEM((block, images), bf16), pltpu.SemaphoreType.DMA((2 * block // LANES,))],
        compiler_params=pltpu.CompilerParams(vmem_limit_bytes=8 * 2**20),
    )(*pinned)


def local(features, prototypes):
    blocks = lax.axis_size("batch")
    block, height = features.shape[0], prototypes.shape[0]
    fits = 4 * blocks * blocks * block * height <= BLOCK_BYTES
    even = block == height and block % (2 * LANES) == 0 and blocks == 4
    if fits and even and lax.axis_size("proto") % 2 == 0 and lax.axis_size("proto") <= 2 * MOST_PARTNERS:
        return whole_plan(features, prototypes)
    return split_plan(features, prototypes)


def solution(mesh):
    in_specs = (P("batch", None), P(("proto", "batch"), None))
    out_specs = P("batch", "proto")
    return jax.shard_map(local, mesh=mesh, in_specs=in_specs, out_specs=out_specs, check_vma=False)
```

```python
import functools

import jax
import jax.numpy as jnp
from jax import lax
from jax.experimental import pallas as pl
from jax.experimental.pallas import tpu as pltpu
from jax.sharding import PartitionSpec as P

ITERS = 3
MOST_PARTNERS = 8
BLOCK_BYTES = 20 * 2**20
VMEM = pltpu.VMEM
IN_VMEM = pl.BlockSpec(memory_space=pltpu.VMEM)
F32 = jnp.float32
LANES = 128


def unit_rows(matrix):
    values = matrix.astype(F32)
    scale = lax.rsqrt(1e-06 + jnp.sum(values * values, axis=1, keepdims=True))
    return (values * scale).astype(jnp.bfloat16)


def partners(size, stride, count, step):
    pairs = []
    for index in range(size):
        place = index // stride % count
        other = place ^ step if count & (count - 1) == 0 else (place + step) % count
        pairs.append((index, index + (other - place) * stride))
    return pairs


def from_others(value, axis, stride, count):
    size = lax.axis_size(axis)
    return [lax.ppermute(value, axis, partners(size, stride, count, step)) for step in range(1, count)]


def swap_cores(value):
    return lax.ppermute(value, "proto", partners(lax.axis_size("proto"), 1, 2, 1))


def group_sum(value, axis, stride, count):
    total = value
    for other in from_others(value, axis, stride, count):
        total = total + other
    return total


def proto_sums(partial_value):
    size = lax.axis_size("batch")
    if size > MOST_PARTNERS:
        return lax.psum(partial_value, "batch")
    return group_sum(partial_value, "batch", 1, size)


def image_sums(partial_value):
    size = lax.axis_size("proto")
    if size > 2 * MOST_PARTNERS or size % 2:
        return lax.psum(partial_value, "proto")
    pair = group_sum(partial_value, "proto", 1, 2)
    return group_sum(pair, "proto", 2, size // 2)


def split_plan(features, prototypes):
    unit_feat = unit_rows(features)
    gathered = lax.all_gather(unit_rows(prototypes), "batch", axis=0, tiled=True)
    scores = jnp.einsum("bd,kd->bk", unit_feat, gathered, preferred_element_type=F32)
    weights = jnp.exp(20.0 * scores)
    total_protos = float(weights.shape[1] * lax.axis_size("proto"))
    row_factor = jnp.ones((weights.shape[0],), F32)
    col_factor = jnp.ones((weights.shape[1],), F32)
    for step in range(ITERS):
        column_part = jnp.dot(row_factor, weights, precision=lax.Precision.HIGHEST)
        col_factor = 1.0 / proto_sums(column_part)
        row_part = jnp.dot(weights, col_factor, precision=lax.Precision.HIGHEST)
        row_factor = 1.0 / image_sums(row_part)
    scaled = weights * row_factor[:, None] * (total_protos * col_factor)[None, :]
    return scaled.astype(jnp.bfloat16)


def call(kernel, outs, args, limit, cost=0, aliases=None, scratch=()):
    pinned = [pltpu.with_memory_space_constraint(arg, VMEM) for arg in args]
    return pl.pallas_call(
        kernel,
        out_shape=[VMEM(shape, dtype) for shape, dtype in outs],
        in_specs=[IN_VMEM] * len(pinned),
        out_specs=[IN_VMEM] * len(outs),
        input_output_aliases=aliases or {},
        scratch_shapes=list(scratch),
        compiler_params=pltpu.CompilerParams(vmem_limit_bytes=limit * 2**20),
        cost_estimate=pl.CostEstimate(flops=max(cost,1), bytes_accessed=1, transcendentals=1),
    )(*pinned)


def scores_of(protos, images):
    return lax.dot_general(protos, images, (((1,), (1,)), ((), ())), preferred_element_type=F32)


def tiles(width):
    return [slice(start, start + LANES) for start in range(0, width, LANES)]


def fill(weights, total, rows, columns, unit_proto, unit_feat):
    step = 2 * LANES
    for column in range(columns.start, columns.stop, step):
        values = jnp.exp(20.0 * scores_of(unit_proto, unit_feat[column : column + step, :]))
        weights[rows, column : column + step] = values
        for tile in tiles(step):
            total = total + values[:, tile]
    return total


def add_images(part, weights, rows, col_factor):
    count = col_factor.shape[0]
    for tile in tiles(part.shape[1]):
        product = weights[rows, tile] * col_factor
        part[:, tile] = part[:, tile] + jnp.sum(product.reshape(count // 8, 8, LANES), axis=0)


def spread(lane_sums):
    return jnp.broadcast_to(1.0 / jnp.sum(lane_sums, axis=1, keepdims=True), lane_sums.shape)


def unit_kernel(feats, protos, unit_feat, unit_proto, raw, sems):
    copies = [pltpu.make_async_copy(src, raw.at[i], sems.at[i]) for i, src in enumerate((feats, protos))]
    for copy in copies:
        copy.start()
    for index, unit in enumerate((unit_feat, unit_proto)):
        copies[index].wait()
        unit[...] = unit_rows(raw[index])


def near_kernel(own_feat, near, near_swapped, own_proto, unit_feat, unit_proto, weights, sums):
    block = own_feat.shape[0]
    core = lax.axis_index("proto") % 2
    unit_feat[:block, :] = own_feat[...]
    unit_feat[pl.ds(pl.multiple_of((1 + core) * block, block), block), :] = unit_rows(near[...])
    unit_feat[pl.ds(pl.multiple_of((2 - core) * block, block), block), :] = unit_rows(near_swapped[...])
    unit_proto[:block, :] = own_proto[...]
    total = jnp.zeros((block, LANES), F32)
    sums[:block, :] = fill(weights, total, slice(0, block), slice(0, 3 * block), own_proto[...], unit_feat)


def first_kernel(first, sums_in, unit_feat, proto_in, weights_in, sums, unit_proto, weights):
    block = first.shape[0]
    rows = slice(block, 2 * block)
    unit_proto[rows, :] = first[...]
    total = jnp.zeros((block, LANES), F32)
    sums[rows, :] = fill(weights, total, rows, slice(0, 3 * block), first[...], unit_feat)


def far_kernel(far, far_swapped, sums, unit_proto, feat_in, weights_in, unit_feat, weights, part):
    half = far.shape[0]
    block = 2 * half
    core = lax.axis_index("proto") % 2
    unit_feat[pl.ds(pl.multiple_of(3 * block + (1 - core) * half, half), half), :] = unit_rows(far[...])
    unit_feat[pl.ds(pl.multiple_of(3 * block + core * half, half), half), :] = unit_rows(far_swapped[...])
    part[...] = jnp.zeros(part.shape, F32)

    def body(index, carry):
        rows = pl.ds(pl.multiple_of(index * block, block), block)
        total = fill(weights, sums[rows, :], rows, slice(3 * block, 4 * block), unit_proto[rows, :], unit_feat)
        add_images(part, weights, rows, spread(total))
        return carry

    lax.fori_loop(0, 2, body, 0)


def more_kernel(start, ready,  unit_feat, proto_in, weights_in, part_in, unit_proto, weights, part, *row_sums):
    rows = slice(start, start + ready.shape[0])
    unit_proto[rows, :] = ready[...]
    total = jnp.zeros((ready.shape[0], LANES), F32)
    total = fill(weights, total, rows, slice(0, weights.shape[1]), unit_proto[rows, :], unit_feat)
    add_images(part, weights, rows, spread(total))
    for store in row_sums:
        store[...] = flat(part)


def flat(part):
    return jnp.sum(part[...], axis=0, keepdims=True)


def summed(parts):
    total = parts[0][...]
    for part in parts[1:]:
        total = total + part[...]
    return total


def pass_kernel(count, block, *refs):
    parts, weights, row_sums, *col_factor, part = refs[:count], *refs[count:]
    row_factor = 1.0 / summed(parts)
    part[...] = jnp.zeros(part.shape, F32)

    def body(index, carry):
        rows = pl.ds(pl.multiple_of(index * block, block), block)
        total = jnp.zeros((block, LANES), F32)
        for tile in tiles(weights.shape[1]):
            total = total + weights[rows, tile] * row_factor[:, tile]
        factor = spread(total)
        for store in col_factor:
            store[rows, :] = factor
        add_images(part, weights, rows, factor)
        return carry

    lax.fori_loop(0, weights.shape[0] // block, body, 0)
    row_sums[...] = flat(part)


def ready_kernel(scale, unit_feat, unit_proto, col_factor, ready):
    block = ready.shape[0]
    images = unit_feat[:block, :]
    for start in range(0, ready.shape[1], block):
        values = jnp.exp(20.0 * scores_of(images, unit_proto[start : start + block, :]))
        for tile in tiles(block):
            at = slice(start + tile.start, start + tile.stop)
            factor = scale * jnp.transpose(col_factor[at, :])[:1, :]
            ready[:, at] = values[:, tile] * factor


def last_kernel(count, block, *refs):
    parts, ready, out, staged, sems = refs[:count], *refs[count:]
    inverse = 1.0 / summed(parts)
    place = lax.axis_index("batch")
    core = lax.axis_index("proto") % 2
    bases = [jnp.bitwise_xor(place, step) * block for step in (0, 1 + core, 2 - core, 3)]
    height = block // sems.shape[0]
    copies = []
    for index in range(sems.shape[0]):
        rows = slice(index * height, (index + 1) * height)
        group = rows.start // LANES * LANES
        spread_rows = jnp.transpose(jnp.broadcast_to(inverse[:, group : group + LANES], (LANES, LANES)))
        factor = spread_rows[rows.start - group : rows.stop - group]
        for number, base in enumerate(bases):
            for tile in tiles(block):
                values = ready[rows, number * block + tile.start : number * block + tile.stop]
                column = pl.multiple_of(base + tile.start, LANES)
                staged[rows, pl.ds(column, LANES)] = (values * factor).astype(staged.dtype)
        copies.append(pltpu.make_async_copy(staged.at[rows], out.at[rows], sems.at[index]))
        copies[-1].start()
    for copy in copies:
        copy.wait()


def by_core(steps):
    protos, blocks = lax.axis_size("proto"), lax.axis_size("batch")
    return [
        (place * protos + proto, (place ^ steps[proto % 2]) * protos + proto)
        for place in range(blocks)
        for proto in range(protos)
    ]


def send(value, steps):
    return lax.ppermute(value, ("batch", "proto"), by_core(steps))


def whole_plan(features, prototypes):
    bf16 = jnp.bfloat16
    blocks = lax.axis_size("batch")
    block, depth = features.shape
    images = blocks * block
    z_count = lax.axis_size("proto") // 2
    total_protos = float(images * lax.axis_size("proto"))
    feat_shape = ((images, depth), bf16)
    weights_shape = ((images, images), F32)
    part_shape = ((8, images), F32)
    lanes_shape = ((images, LANES), F32)

    half = block // 2
    core = lax.axis_index("proto") % 2
    own_feat, own_proto = pl.pallas_call(
        unit_kernel,
        out_shape=[VMEM((block, depth), bf16)] * 2,
        in_specs=[pl.BlockSpec(memory_space=pltpu.HBM)] * 2,
        out_specs=[IN_VMEM] * 2,
        scratch_shapes=[VMEM((2, block, depth), bf16), pltpu.SemaphoreType.DMA((2,))],
        compiler_params=pltpu.CompilerParams(vmem_limit_bytes=4 * 2**20),
        cost_estimate=pl.CostEstimate(flops=1, bytes_accessed=1, transcendentals=1),
    )(*[pltpu.with_memory_space_constraint(arg, pltpu.HBM) for arg in (features, prototypes)])
    near = send(features, (1, 2))
    first = send(own_proto, (1, 2))
    second = send(own_proto, (2, 1))
    near_half = lax.dynamic_slice_in_dim(near, (1 - core) * half, half, 0)
    forward, own_feat, own_proto = lax.optimization_barrier((near_half, own_feat, own_proto))
    far = send(forward, (2, 1))
    unit_feat, unit_proto, weights, sums = call(
        near_kernel,
        [feat_shape, feat_shape, weights_shape, lanes_shape],
        [own_feat, near, swap_cores(near), own_proto],
        16,
    )
    far, sums = lax.optimization_barrier((far, sums))
    cut = 9 * block // 16
    last = [send(first[:cut], (2, 1)), send(first[cut:], (2, 1))]
    sums, unit_proto, weights = call(
        first_kernel,
        [lanes_shape, feat_shape, weights_shape],
        [first, sums, unit_feat, unit_proto, weights],
        16,
        aliases={1: 0, 3: 1, 4: 2},
    )
    unit_feat, weights, part = call(
        far_kernel,
        [feat_shape, weights_shape, part_shape],
        [far, swap_cores(far), sums, unit_proto, unit_feat, weights],
        16,
        aliases={4: 0, 5: 1},
    )
    outs = [feat_shape, weights_shape, part_shape, ((1, images), F32)]
    start = 2 * block
    for piece in (second, *last):
        end = start + piece.shape[0]
        unit_proto, weights, part, *row_sums = call(
            functools.partial(more_kernel, start),
            outs if end == images else outs[:3],
            [piece, unit_feat, unit_proto, weights, part],
            16,
            aliases={2: 0, 3: 1, 4: 2},
        )
        start = end

    def around(value):
        total = value + swap_cores(value)
        *others, nearest = reversed(from_others(total, "proto", 2, z_count))
        for other in others:
            total = lax.optimization_barrier(total + other)
        return [total, nearest]

    parts = around(*row_sums)
    for step in range(1, ITERS):
        final = step == ITERS - 1
        wanted = block if final else images
        row_sums, *col_factor = call(
            functools.partial(pass_kernel, len(parts), block),
            [((1, wanted), F32), lanes_shape] if final else [((1, wanted), F32)],
            [*parts, weights],
            8,
            cost=4 * images * images,
            scratch=[VMEM((8, wanted), F32)],
        )
        parts = around(row_sums)
    (ready,) = call(
        functools.partial(ready_kernel, total_protos),
        [((block, images), F32)],
        [unit_feat, unit_proto, *col_factor],
        16,
        cost=2 * block * images * depth,
    )
    pinned = [pltpu.with_memory_space_constraint(arg, VMEM) for arg in [*parts, ready]]
    return pl.pallas_call(
        functools.partial(last_kernel, len(parts), block),
        out_shape=jax.ShapeDtypeStruct((block, images), bf16),
        in_specs=[IN_VMEM] * len(pinned),
        out_specs=pl.BlockSpec(memory_space=pl.ANY),
        scratch_shapes=[VMEM((block, images), bf16), pltpu.SemaphoreType.DMA((2 * block // LANES,))],
        compiler_params=pltpu.CompilerParams(vmem_limit_bytes=8 * 2**20),
    )(*pinned)


def local(features, prototypes):
    blocks = lax.axis_size("batch")
    block, height = features.shape[0], prototypes.shape[0]
    fits = 4 * blocks * blocks * block * height <= BLOCK_BYTES
    even = block == height and block % (2 * LANES) == 0 and blocks == 4
    if fits and even and lax.axis_size("proto") % 2 == 0 and lax.axis_size("proto") <= 2 * MOST_PARTNERS:
        return whole_plan(features, prototypes)
    return split_plan(features, prototypes)


def solution(mesh):
    in_specs = (P("batch", None), P(("proto", "batch"), None))
    out_specs = P("batch", "proto")
    return jax.shard_map(local, mesh=mesh, in_specs=in_specs, out_specs=out_specs, check_vma=False)
```

```python
import functools

import jax
import jax.numpy as jnp
from jax import lax
from jax.experimental import pallas as pl
from jax.experimental.pallas import tpu as pltpu
from jax.sharding import PartitionSpec as P

ITERS = 3
MOST_PARTNERS = 8
BLOCK_BYTES = 20 * 2**20
VMEM = pltpu.VMEM
IN_VMEM = pl.BlockSpec(memory_space=pltpu.VMEM)
F32 = jnp.float32
LANES = 128


def unit_rows(matrix):
    values = matrix.astype(F32)
    scale = lax.rsqrt(1e-06 + jnp.sum(values * values, axis=1, keepdims=True))
    return (values * scale).astype(jnp.bfloat16)


def partners(size, stride, count, step):
    pairs = []
    for index in range(size):
        place = index // stride % count
        other = place ^ step if count & (count - 1) == 0 else (place + step) % count
        pairs.append((index, index + (other - place) * stride))
    return pairs


def from_others(value, axis, stride, count):
    size = lax.axis_size(axis)
    return [lax.ppermute(value, axis, partners(size, stride, count, step)) for step in range(1, count)]


def swap_cores(value):
    return lax.ppermute(value, "proto", partners(lax.axis_size("proto"), 1, 2, 1))


def group_sum(value, axis, stride, count):
    total = value
    for other in from_others(value, axis, stride, count):
        total = total + other
    return total


def proto_sums(partial_value):
    size = lax.axis_size("batch")
    if size > MOST_PARTNERS:
        return lax.psum(partial_value, "batch")
    return group_sum(partial_value, "batch", 1, size)


def image_sums(partial_value):
    size = lax.axis_size("proto")
    if size > 2 * MOST_PARTNERS or size % 2:
        return lax.psum(partial_value, "proto")
    pair = group_sum(partial_value, "proto", 1, 2)
    return group_sum(pair, "proto", 2, size // 2)


def split_plan(features, prototypes):
    unit_feat = unit_rows(features)
    gathered = lax.all_gather(unit_rows(prototypes), "batch", axis=0, tiled=True)
    scores = jnp.einsum("bd,kd->bk", unit_feat, gathered, preferred_element_type=F32)
    weights = jnp.exp(20.0 * scores)
    total_protos = float(weights.shape[1] * lax.axis_size("proto"))
    row_factor = jnp.ones((weights.shape[0],), F32)
    col_factor = jnp.ones((weights.shape[1],), F32)
    for step in range(ITERS):
        column_part = jnp.dot(row_factor, weights, precision=lax.Precision.HIGHEST)
        col_factor = 1.0 / proto_sums(column_part)
        row_part = jnp.dot(weights, col_factor, precision=lax.Precision.HIGHEST)
        row_factor = 1.0 / image_sums(row_part)
    scaled = weights * row_factor[:, None] * (total_protos * col_factor)[None, :]
    return scaled.astype(jnp.bfloat16)


def call(kernel, outs, args, limit, cost=0, aliases=None, scratch=()):
    pinned = [pltpu.with_memory_space_constraint(arg, VMEM) for arg in args]
    return pl.pallas_call(
        kernel,
        out_shape=[VMEM(shape, dtype) for shape, dtype in outs],
        in_specs=[IN_VMEM] * len(pinned),
        out_specs=[IN_VMEM] * len(outs),
        input_output_aliases=aliases or {},
        scratch_shapes=list(scratch),
        compiler_params=pltpu.CompilerParams(vmem_limit_bytes=limit * 2**20),
        cost_estimate=pl.CostEstimate(flops=max(cost,1), bytes_accessed=1, transcendentals=1),
    )(*pinned)


def scores_of(protos, images):
    return lax.dot_general(protos, images, (((1,), (1,)), ((), ())), preferred_element_type=F32)


def tiles(width):
    return [slice(start, start + LANES) for start in range(0, width, LANES)]


def fill(weights, total, rows, columns, unit_proto, unit_feat):
    step = 2 * LANES
    for column in range(columns.start, columns.stop, step):
        values = jnp.exp(20.0 * scores_of(unit_proto, unit_feat[column : column + step, :]))
        weights[rows, column : column + step] = values
        for tile in tiles(step):
            total = total + values[:, tile]
    return total


def add_images(part, weights, rows, col_factor):
    count = col_factor.shape[0]
    for tile in tiles(part.shape[1]):
        product = weights[rows, tile] * col_factor
        part[:, tile] = part[:, tile] + jnp.sum(product.reshape(count // 8, 8, LANES), axis=0)


def spread(lane_sums):
    return jnp.broadcast_to(1.0 / jnp.sum(lane_sums, axis=1, keepdims=True), lane_sums.shape)


def unit_kernel(feats, protos, unit_feat, unit_proto, raw, sems):
    copies = [pltpu.make_async_copy(src, raw.at[i], sems.at[i]) for i, src in enumerate((feats, protos))]
    for copy in copies:
        copy.start()
    for index, unit in enumerate((unit_feat, unit_proto)):
        copies[index].wait()
        unit[...] = unit_rows(raw[index])


def near_kernel(own_feat, near, near_swapped, own_proto, unit_feat, unit_proto, weights, sums):
    block = own_feat.shape[0]
    core = lax.axis_index("proto") % 2
    unit_feat[:block, :] = own_feat[...]
    unit_feat[pl.ds(pl.multiple_of((1 + core) * block, block), block), :] = unit_rows(near[...])
    unit_feat[pl.ds(pl.multiple_of((2 - core) * block, block), block), :] = unit_rows(near_swapped[...])
    unit_proto[:block, :] = own_proto[...]
    total = jnp.zeros((block, LANES), F32)
    sums[:block, :] = fill(weights, total, slice(0, block), slice(0, 3 * block), own_proto[...], unit_feat)


def first_kernel(first, sums_in, unit_feat, proto_in, weights_in, sums, unit_proto, weights):
    block = first.shape[0]
    rows = slice(block, 2 * block)
    unit_proto[rows, :] = first[...]
    total = jnp.zeros((block, LANES), F32)
    sums[rows, :] = fill(weights, total, rows, slice(0, 3 * block), first[...], unit_feat)


def far_kernel(far, *refs):
    *far_swapped, sums, unit_proto, feat_in, weights_in, unit_feat, weights, part = refs
    half = far.shape[0]
    block = 2 * half
    core = lax.axis_index("proto") % 2
    unit_feat[pl.ds(pl.multiple_of(3 * block + (1 - core) * half, half), half), :] = unit_rows(far[...])
    height = half // len(far_swapped)
    for index, piece in enumerate(far_swapped):
        start = pl.multiple_of(3 * block + core * half + index * height, height)
        unit_feat[pl.ds(start, height), :] = unit_rows(piece[...])
    part[...] = jnp.zeros(part.shape, F32)

    def body(index, carry):
        rows = pl.ds(pl.multiple_of(index * block, block), block)
        total = fill(weights, sums[rows, :], rows, slice(3 * block, 4 * block), unit_proto[rows, :], unit_feat)
        add_images(part, weights, rows, spread(total))
        return carry

    lax.fori_loop(0, 2, body, 0)


def more_kernel(start, ready,  unit_feat, proto_in, weights_in, part_in, unit_proto, weights, part, *row_sums):
    rows = slice(start, start + ready.shape[0])
    unit_proto[rows, :] = ready[...]
    total = jnp.zeros((ready.shape[0], LANES), F32)
    total = fill(weights, total, rows, slice(0, weights.shape[1]), unit_proto[rows, :], unit_feat)
    add_images(part, weights, rows, spread(total))
    for store in row_sums:
        store[...] = flat(part)


def flat(part):
    return jnp.sum(part[...], axis=0, keepdims=True)


def summed(parts):
    total = parts[0][...]
    for part in parts[1:]:
        total = total + part[...]
    return total


def pass_kernel(count, block, *refs):
    parts, weights, row_sums, *col_factor, part = refs[:count], *refs[count:]
    row_factor = 1.0 / summed(parts)
    part[...] = jnp.zeros(part.shape, F32)

    def body(index, carry):
        rows = pl.ds(pl.multiple_of(index * block, block), block)
        total = jnp.zeros((block, LANES), F32)
        for tile in tiles(weights.shape[1]):
            total = total + weights[rows, tile] * row_factor[:, tile]
        factor = spread(total)
        for store in col_factor:
            store[rows, :] = factor
        add_images(part, weights, rows, factor)
        return carry

    lax.fori_loop(0, weights.shape[0] // block, body, 0)
    row_sums[...] = flat(part)


def ready_kernel(scale, unit_feat, unit_proto, col_factor, ready):
    block = ready.shape[0]
    images = unit_feat[:block, :]
    for start in range(0, ready.shape[1], block):
        values = jnp.exp(20.0 * scores_of(images, unit_proto[start : start + block, :]))
        for tile in tiles(block):
            at = slice(start + tile.start, start + tile.stop)
            factor = scale * jnp.transpose(col_factor[at, :])[:1, :]
            ready[:, at] = values[:, tile] * factor


def last_kernel(count, block, *refs):
    parts, ready, out, staged, sems = refs[:count], *refs[count:]
    inverse = 1.0 / summed(parts)
    place = lax.axis_index("batch")
    core = lax.axis_index("proto") % 2
    bases = [jnp.bitwise_xor(place, step) * block for step in (0, 1 + core, 2 - core, 3)]
    height = block // sems.shape[0]
    copies = []
    for index in range(sems.shape[0]):
        rows = slice(index * height, (index + 1) * height)
        group = rows.start // LANES * LANES
        spread_rows = jnp.transpose(jnp.broadcast_to(inverse[:, group : group + LANES], (LANES, LANES)))
        factor = spread_rows[rows.start - group : rows.stop - group]
        for number, base in enumerate(bases):
            for tile in tiles(block):
                values = ready[rows, number * block + tile.start : number * block + tile.stop]
                column = pl.multiple_of(base + tile.start, LANES)
                staged[rows, pl.ds(column, LANES)] = (values * factor).astype(staged.dtype)
        copies.append(pltpu.make_async_copy(staged.at[rows], out.at[rows], sems.at[index]))
        copies[-1].start()
    for copy in copies:
        copy.wait()


def by_core(steps):
    protos, blocks = lax.axis_size("proto"), lax.axis_size("batch")
    return [
        (place * protos + proto, (place ^ steps[proto % 2]) * protos + proto)
        for place in range(blocks)
        for proto in range(protos)
    ]


def send(value, steps):
    return lax.ppermute(value, ("batch", "proto"), by_core(steps))


def whole_plan(features, prototypes):
    bf16 = jnp.bfloat16
    blocks = lax.axis_size("batch")
    block, depth = features.shape
    images = blocks * block
    z_count = lax.axis_size("proto") // 2
    total_protos = float(images * lax.axis_size("proto"))
    feat_shape = ((images, depth), bf16)
    weights_shape = ((images, images), F32)
    part_shape = ((8, images), F32)
    lanes_shape = ((images, LANES), F32)

    half = block // 2
    core = lax.axis_index("proto") % 2
    own_feat, own_proto = pl.pallas_call(
        unit_kernel,
        out_shape=[VMEM((block, depth), bf16)] * 2,
        in_specs=[pl.BlockSpec(memory_space=pltpu.HBM)] * 2,
        out_specs=[IN_VMEM] * 2,
        scratch_shapes=[VMEM((2, block, depth), bf16), pltpu.SemaphoreType.DMA((2,))],
        compiler_params=pltpu.CompilerParams(vmem_limit_bytes=4 * 2**20),
        cost_estimate=pl.CostEstimate(flops=1, bytes_accessed=1, transcendentals=1),
    )(*[pltpu.with_memory_space_constraint(arg, pltpu.HBM) for arg in (features, prototypes)])
    near = send(features, (1, 2))
    first = send(own_proto, (1, 2))
    second = send(own_proto, (2, 1))
    near_half = lax.dynamic_slice_in_dim(near, (1 - core) * half, half, 0)
    forward, own_feat, own_proto = lax.optimization_barrier((near_half, own_feat, own_proto))
    far = send(forward, (2, 1))
    unit_feat, unit_proto, weights, sums = call(
        near_kernel,
        [feat_shape, feat_shape, weights_shape, lanes_shape],
        [own_feat, near, swap_cores(near), own_proto],
        16,
    )
    far, sums = lax.optimization_barrier((far, sums))
    cut = 5 * block // 8
    last = [send(first[:cut], (2, 1)), send(first[cut:], (2, 1))]
    sums, unit_proto, weights = call(
        first_kernel,
        [lanes_shape, feat_shape, weights_shape],
        [first, sums, unit_feat, unit_proto, weights],
        16,
        aliases={1: 0, 3: 1, 4: 2},
    )
    swapped = [swap_cores(far[: half // 2]), swap_cores(far[half // 2 :])]
    unit_feat, weights, part = call(
        far_kernel,
        [feat_shape, weights_shape, part_shape],
        [far, *swapped, sums, unit_proto, unit_feat, weights],
        16,
        aliases={3 + len(swapped): 0, 4 + len(swapped): 1},
    )
    outs = [feat_shape, weights_shape, part_shape, ((1, images), F32)]
    start = 2 * block
    for piece in (second, *last):
        end = start + piece.shape[0]
        unit_proto, weights, part, *row_sums = call(
            functools.partial(more_kernel, start),
            outs if end == images else outs[:3],
            [piece, unit_feat, unit_proto, weights, part],
            16,
            aliases={2: 0, 3: 1, 4: 2},
        )
        start = end

    def around(value):
        total = value + swap_cores(value)
        far, *others = reversed(from_others(total, "proto", 2, z_count))
        total = lax.optimization_barrier(total + far)
        for other in others[:-1]:
            total = lax.optimization_barrier(total + other)
        return [total, others[-1]]

    parts = around(*row_sums)
    for step in range(1, ITERS):
        final = step == ITERS - 1
        wanted = block if final else images
        row_sums, *col_factor = call(
            functools.partial(pass_kernel, len(parts), block),
            [((1, wanted), F32), lanes_shape] if final else [((1, wanted), F32)],
            [*parts, weights],
            8,
            cost=4 * images * images,
            scratch=[VMEM((8, wanted), F32)],
        )
        parts = around(row_sums)
    (ready,) = call(
        functools.partial(ready_kernel, total_protos),
        [((block, images), F32)],
        [unit_feat, unit_proto, *col_factor],
        16,
        cost=2 * block * images * depth,
    )
    pinned = [pltpu.with_memory_space_constraint(arg, VMEM) for arg in [*parts, ready]]
    return pl.pallas_call(
        functools.partial(last_kernel, len(parts), block),
        out_shape=jax.ShapeDtypeStruct((block, images), bf16),
        in_specs=[IN_VMEM] * len(pinned),
        out_specs=pl.BlockSpec(memory_space=pl.ANY),
        scratch_shapes=[VMEM((block, images), bf16), pltpu.SemaphoreType.DMA((2 * block // LANES,))],
        compiler_params=pltpu.CompilerParams(vmem_limit_bytes=8 * 2**20),
    )(*pinned)


def local(features, prototypes):
    blocks = lax.axis_size("batch")
    block, height = features.shape[0], prototypes.shape[0]
    fits = 4 * blocks * blocks * block * height <= BLOCK_BYTES
    even = block == height and block % (2 * LANES) == 0 and blocks == 4
    if fits and even and lax.axis_size("proto") % 2 == 0 and lax.axis_size("proto") <= 2 * MOST_PARTNERS:
        return whole_plan(features, prototypes)
    return split_plan(features, prototypes)


def solution(mesh):
    in_specs = (P("batch", None), P(("proto", "batch"), None))
    out_specs = P("batch", "proto")
    return jax.shard_map(local, mesh=mesh, in_specs=in_specs, out_specs=out_specs, check_vma=False)
```
